32 devices in a mesh: row: 8 (over y, x, core), col: 4 (over z).
Axes of the slice: x: 2, y: 2, z: 4, core: 2. Of those that a mesh axis runs over, the one named last changes fastest.
Arguments:
- parent_inverse: float32 [24576, 24576], P('row', 'col'), may hold values from -6 to 6
- panel: float32 [24576, 1024], P(('col', 'row')), may hold values from -0.0390625 to 0.0390625
- saved_diag: float32 [1024, 1024], P('row', 'col'), may hold values from -6 to 6
Outputs:
- offdiag_block: float32 [24576, 1024], P(('row', 'col'))
- diag_block: float32 [1024, 1024], P('row', 'col')
The draws below stay inside these ranges and needn't reach their ends.
All inputs are finite; a program needn't handle non-finite values.
Results may differ from the reference program's by a relative error of at most 0.00007.
Values sent between devices are 32-bit elements; how exact they have to be, the bound alone decides.
No kernel may reach another device: no remote copies, remote signals or barrier semaphores. Data moves between devices by JAX's collectives and lax.ppermute only.
A program may use at most 192 MiB of HBM per device.

```python
import jax
import jax.numpy as jnp
from jax import lax

B = 24576
P_SIZE = 1024


def block_scale(rng, shape, pieces, smallest, largest):
    def one(position, parts):
        heights = jax.random.uniform(jax.random.fold_in(jax.random.fold_in(rng, 6), position), (parts,), jnp.float32, smallest / len(pieces), largest / len(pieces))
        return jnp.repeat(jnp.exp(heights), shape[position] // parts).reshape((-1,) + (1,) * (len(shape) - position - 1))

    level = one(*pieces[0])
    for cut in pieces[1:]:
        level = level * one(*cut)
    return level


def gaussian(rng, extent, spread, bound, split=(), dtype=jnp.bfloat16):
    drawn = spread * jax.random.normal(rng, extent, jnp.float32)
    if split:
        drawn = drawn * block_scale(rng, extent, split, -0.22, 0.18)
    return jnp.clip(drawn, -bound, bound).astype(dtype)


def setup_inputs(seed: int = 0) -> dict:
    seeds = jax.random.split(jax.random.key(seed), 4)
    return {
        "parent_inverse": gaussian(seeds[0], (B, B), 1.0, 6.0, ((0, 8), (1, 4)), jnp.float32),
        "panel": gaussian(seeds[1], (B, P_SIZE), B ** -0.5, 0.0390625, ((0, 32),), jnp.float32),
        "saved_diag": gaussian(seeds[2], (P_SIZE, P_SIZE), 1.0, 6.0, ((0, 8), (1, 4)), jnp.float32),
    }


def reference(parent_inverse, panel, saved_diag):
    product = jnp.dot(parent_inverse, panel, precision=lax.Precision.HIGHEST, preferred_element_type=jnp.float32)
    offdiag_block = -product
    gram = jnp.dot(panel.T, product, precision=lax.Precision.HIGHEST, preferred_element_type=jnp.float32)
    diag_block = saved_diag + gram
    return offdiag_block, diag_block
```

```python
import functools

import jax
import jax.numpy as jnp
import numpy as np
from jax import lax
from jax.experimental import pallas as pl
from jax.experimental.pallas import tpu as pltpu
from jax.sharding import PartitionSpec as P

CHUNKS = 4
PARTS = 2
MIB = 1 << 20


def split(value):
    high = value.astype(jnp.bfloat16)
    low = (value - high.astype(jnp.float32)).astype(jnp.bfloat16)
    return high, low


def largest_divisor(extent, unit, limit):
    return max(d for d in range(unit, min(extent, limit) + 1, unit) if extent % d == 0)


def product_kernel(depth, block, place_ref, a_ref, *refs):
    pieces, (out_ref, high_ref, low_ref) = refs[:-3], refs[-3:]

    @pl.when(pl.program_id(0) == 0)
    def _():
        slot = 0
        for piece in pieces:
            for part in range(piece.shape[0] // block):
                high, low = split(piece[pl.ds(part * block, block), :])
                rows = pl.ds(pl.multiple_of(place_ref[slot] * block, block), block)
                high_ref[rows, :] = high
                low_ref[rows, :] = low
                slot += 1

    dot = functools.partial(jnp.dot, preferred_element_type=jnp.float32)

    def term(index):
        span = pl.ds(pl.multiple_of(index * depth, depth), depth)
        a_high, a_low = split(-a_ref[:, span])
        b_high, b_low = high_ref[span, :], low_ref[span, :]
        return dot(a_high, b_high) + (dot(a_low, b_high) + dot(a_high, b_low))

    def body(index, carry):
        out_ref[...] += term(index)
        return carry

    out_ref[...] = term(0)
    lax.fori_loop(1, a_ref.shape[1] // depth, body, 0)


def negative_product(a, pieces, place, tile, part):
    rows, inner = a.shape
    columns = pieces[0].shape[1]
    block = inner // place.shape[0]
    depth = largest_divisor(inner, 256, 1024)
    whole = [pl.BlockSpec(piece.shape, lambda i, _: (0, 0), pipeline_mode=pl.Buffered(1)) for piece in pieces]
    rows //= PARTS
    return pl.pallas_call(
        functools.partial(product_kernel, depth, block),
        grid_spec=pltpu.PrefetchScalarGridSpec(
            num_scalar_prefetch=1,
            grid=(rows // tile,),
            in_specs=[pl.BlockSpec((tile, inner), lambda i, _: (i * PARTS + part, 0))] + whole,
            out_specs=pl.BlockSpec((tile, columns), lambda i, _: (i, 0)),
            scratch_shapes=[pltpu.VMEM((inner, columns), jnp.bfloat16)] * 2,
        ),
        out_shape=jax.ShapeDtypeStruct((rows, columns), jnp.float32),
        compiler_params=pltpu.CompilerParams(vmem_limit_bytes=40 * MIB, dimension_semantics=("arbitrary",)),
        cost_estimate=pl.CostEstimate(
            flops=6 * rows * inner * columns,
            bytes_accessed=4 * (rows * inner + inner * columns + rows * columns),
            transcendentals=0,
        ),
    )(place, a, *pieces)


def gather_orders(count):
    masks = [1 << b for b in range(1, count.bit_length() - 1)]
    return masks, masks[::-1]


def gather_places(count):
    orders = gather_orders(count)
    held = [[i] for i in range(count)]
    for step in range(len(orders[0])):
        held = [held[i] + held[i ^ orders[i & 1][step]] for i in range(count)]
    return np.array([held[i] + held[i ^ 1] for i in range(count)], np.int32)


def after(value, *others):
    return lax.optimization_barrier((value, *others))[0]


def cross(pieces, masks, count):
    pairs = [(i, i ^ masks[i & 1]) for i in range(count)]
    return [lax.ppermute(piece, "row", pairs) for piece in pieces]


def sum_over_row(value, count):
    rows, columns = value.shape
    me = lax.axis_index("row")
    value = value.reshape((2,) * (count.bit_length() - 1) + (rows // count, columns))
    for bit in range(count.bit_length() - 1):
        axis = value.ndim - 3
        mine = (me >> bit) & 1
        keep = lax.dynamic_index_in_dim(value, mine, axis, keepdims=False)
        send = lax.dynamic_index_in_dim(value, 1 - mine, axis, keepdims=False)
        value = keep + lax.ppermute(send, "row", [(i, i ^ (1 << bit)) for i in range(count)])
    return value


def sum_over_col(value, count):
    me = lax.axis_index("col")
    width = value.shape[1] // count
    total = lax.dynamic_slice_in_dim(value, me * width, width, 1)
    for shift in range(1, count):
        send = lax.dynamic_slice_in_dim(value, (me + shift) % count * width, width, 1)
        total = total + lax.ppermute(send, "col", [(i, (i + shift) % count) for i in range(count)])
    return total


def shards(parent_inverse, panel, saved_diag):
    row_count, column_count = lax.axis_size("row"), lax.axis_size("col")
    width = panel.shape[1] // CHUNKS
    tile = parent_inverse.shape[0] // column_count // PARTS
    place = jnp.asarray(gather_places(row_count))[lax.axis_index("row")]
    steps = list(zip(*gather_orders(row_count))) + [(1, 1)]
    pairs = [
        (r * column_count + c, c * row_count + r) for r in range(row_count) for c in range(column_count)
    ]

    def gather_step(pieces, step, last):
        return pieces + cross([after(pieces[0], last)] + pieces[1:], steps[step], row_count)

    pieces = [lax.slice_in_dim(panel, 0, width, axis=1)]
    for step in range(len(steps)):
        pieces = pieces + cross(pieces, steps[step], row_count)
    own_rows = lax.ppermute(after(panel, pieces[-1]), ("row", "col"), pairs)
    partials = []
    for chunk in range(CHUNKS):
        following = [lax.slice_in_dim(panel, (chunk + 1) * width, (chunk + 2) * width, axis=1)] if chunk + 1 < CHUNKS else []
        last = pieces[-1]
        for part in range(PARTS):
            if chunk + 1 < CHUNKS:
                for step in range(part * (len(steps) - 1) // PARTS, (part + 1) * (len(steps) - 1) // PARTS):
                    following = gather_step(following, step, last)
            last = negative_product(after(parent_inverse, last), pieces, place, tile, part)
            partials.append(last)
        if chunk + 1 < CHUNKS:
            following = gather_step(following, len(steps) - 1, last)
        pieces = following
    blocks, grams = [], []
    for chunk in range(CHUNKS):
        halves = [
            lax.psum_scatter(partials[chunk * PARTS + part], "col", scatter_dimension=0, tiled=True)
            for part in range(PARTS)
        ]
        block = jnp.concatenate(halves, axis=0)
        gram = lax.dot_general(
            own_rows,
            after(block, partials[min(PARTS * CHUNKS, (chunk + 3) * PARTS) - 1]),
            (((0,), (0,)), ((), ())),
            precision=lax.Precision.HIGH,
            preferred_element_type=jnp.float32,
        )
        blocks.append(block)
        grams.append(sum_over_row(gram, row_count))
    offdiag_block = jnp.concatenate(blocks, axis=1)
    diag_block = saved_diag - sum_over_col(jnp.concatenate(grams, axis=1), column_count)
    return offdiag_block, diag_block


def solution(mesh):
    in_specs = (P("row", "col"), P(("col", "row"), None), P("row", "col"))
    out_specs = (P(("row", "col"), None), P("row", "col"))
    return jax.shard_map(shards, mesh=mesh, in_specs=in_specs, out_specs=out_specs, check_vma=False)
```

```python
import functools

import jax
import jax.numpy as jnp
import numpy as np
from jax import lax
from jax.experimental import pallas as pl
from jax.experimental.pallas import tpu as pltpu
from jax.sharding import PartitionSpec as P

CHUNKS = 4
LANES = 128
MIB = 1 << 20


def split(value):
    high = value.astype(jnp.bfloat16)
    low = (value - high.astype(jnp.float32)).astype(jnp.bfloat16)
    return high, low


def largest_divisor(extent, unit, limit):
    return max(d for d in range(unit, min(extent, limit) + 1, unit) if extent % d == 0)


def product_kernel(count, place_ref, a_ref, *refs):
    del place_ref
    pieces, sums, (out_ref, high_ref, low_ref) = refs[:count], refs[count:-3], refs[-3:]
    step = pl.program_id(1)

    for slot, piece in enumerate(pieces):

        @pl.when((pl.program_id(0) == 0) & (step == slot))
        def _():
            high_ref[slot], low_ref[slot] = split(-piece[...])

    @pl.when(step == 0)
    def _():
        out_ref[...] = sums[0][...] if sums else jnp.zeros_like(out_ref)

    dot = functools.partial(jnp.dot, preferred_element_type=jnp.float32)
    extent = largest_divisor(a_ref.shape[0], 16, 256)
    for first in range(0, a_ref.shape[0], extent):
        rows = pl.ds(first, extent)
        high, low = split(a_ref[rows, :])
        both = dot(jnp.concatenate([high, low], axis=0), high_ref[step])
        out_ref[rows, :] += both[:extent] + (both[extent:] + dot(high, low_ref[step]))


def negative_product(a, pieces, place, sums=None):
    rows = a.shape[0]
    depth, columns = pieces[0].shape
    tile = largest_divisor(rows, 16, 768)
    out_spec = pl.BlockSpec((tile, columns), lambda i, k, _: (i, 0))
    whole = [pl.BlockSpec(piece.shape, lambda i, k, _: (0, 0), pipeline_mode=pl.Buffered(1)) for piece in pieces]
    given = [] if sums is None else [sums]
    return pl.pallas_call(
        functools.partial(product_kernel, len(pieces)),
        grid_spec=pltpu.PrefetchScalarGridSpec(
            num_scalar_prefetch=1,
            grid=(rows // tile, len(pieces)),
            in_specs=[pl.BlockSpec((tile, depth), lambda i, k, place: (i, place[k]))] + whole + [out_spec] * len(given),
            out_specs=out_spec,
            scratch_shapes=[pltpu.VMEM((len(pieces), depth, columns), jnp.bfloat16)] * 2,
        ),
        out_shape=jax.ShapeDtypeStruct((rows, columns), jnp.float32),
        compiler_params=pltpu.CompilerParams(
            vmem_limit_bytes=40 * MIB, dimension_semantics=("arbitrary", "arbitrary")
        ),
        cost_estimate=pl.CostEstimate(
            flops=6 * rows * depth * len(pieces) * columns,
            bytes_accessed=4 * (rows * depth * len(pieces) + depth * len(pieces) * columns + 2 * rows * columns),
            transcendentals=0,
        ),
    )(place, a, *pieces, *given)


def gather_orders(count):
    masks = [1 << b for b in range(1, count.bit_length() - 1)]
    return list(zip(masks, masks[::-1]))


def gather_places(count):
    held = [[i] for i in range(count)]
    for masks in gather_orders(count):
        held = [held[i] + held[i ^ masks[i & 1]] for i in range(count)]
    half = count // 4
    both = [
        held[i][:half] + held[i ^ 1][:half] + held[i][half:] + held[i ^ 1][half:] for i in range(count)
    ]
    return np.array(both, np.int32)


def after(value, *others):
    return lax.optimization_barrier((value, *others))[0]


def cross(pieces, masks, count):
    pairs = [(i, i ^ masks[i & 1]) for i in range(count)]
    return [lax.ppermute(piece, "row", pairs) for piece in pieces]


def sum_over_row(value, count):
    rows, columns = value.shape
    me = lax.axis_index("row")
    value = value.reshape((2,) * (count.bit_length() - 1) + (rows // count, columns))
    for bit in range(count.bit_length() - 1):
        axis = value.ndim - 3
        mine = (me >> bit) & 1
        keep = lax.dynamic_index_in_dim(value, mine, axis, keepdims=False)
        send = lax.dynamic_index_in_dim(value, 1 - mine, axis, keepdims=False)
        value = keep + lax.ppermute(send, "row", [(i, i ^ (1 << bit)) for i in range(count)])
    return value


def sum_over_col(value, count):
    me = lax.axis_index("col")
    width = value.shape[1] // count
    total = lax.dynamic_slice_in_dim(value, me * width, width, 1)
    for shift in range(1, count):
        send = lax.dynamic_slice_in_dim(value, (me + shift) % count * width, width, 1)
        total = total + lax.ppermute(send, "col", [(i, (i + shift) % count) for i in range(count)])
    return total


def move(value, target):
    row_count, column_count = lax.axis_size("row"), lax.axis_size("col")
    pairs = []
    for r in range(row_count):
        for c in range(column_count):
            to_row, to_column = target(r, c)
            pairs.append((r * column_count + c, to_row * column_count + to_column))
    return lax.ppermute(value, ("row", "col"), pairs)


def shards(parent_inverse, panel, saved_diag):
    row_count, column_count = lax.axis_size("row"), lax.axis_size("col")
    row_index, column_index = lax.axis_index("row"), lax.axis_index("col")
    group = row_count // column_count
    block_rows = panel.shape[0]
    width = panel.shape[1] // CHUNKS
    stepwise = block_rows % LANES == 0
    orders = gather_orders(row_count)
    places = gather_places(row_count)
    place = jnp.asarray(places)[row_index]
    slots = jnp.asarray(np.argsort(places, axis=1).astype(np.int32))[row_index]

    def cut(chunk):
        return lax.slice_in_dim(panel, chunk * width, (chunk + 1) * width, axis=1)

    def partner(pieces):
        return cross(pieces, (1, 1), row_count)

    def early(chunk, last):
        pieces = [cut(chunk) if last is None else after(cut(chunk), last)]
        for masks in orders[:-1]:
            pieces = pieces + cross(pieces, masks, row_count)
        return pieces, pieces + partner(pieces)

    def spread(chunk, select):
        wanted = row_index % group * column_count + (column_index ^ (row_index // group) ^ (chunk % column_count))
        return move(select(wanted), lambda r, c: (r, c ^ (r // group) ^ (chunk % column_count)))

    def hop(value, chunk):
        return move(
            value, lambda r, c: (((r // group) ^ c ^ (chunk % column_count)) * group + r % group, c)
        )

    blocks, own_rows = [], []

    def held_back(chunk):
        return after(parent_inverse, blocks[chunk - 2]) if chunk >= 2 else parent_inverse

    def summed(partial_block):
        return lax.psum_scatter(partial_block, "col", scatter_dimension=0, tiled=True)

    waiting = None
    last = None
    if stepwise:
        half = row_count // 2
        following = early(0, None)
        for chunk in range(CHUNKS):
            mine, first = following
            others = cross([mine[0] if last is None else after(mine[0], last)] + mine[1:], orders[-1], row_count)
            last = negative_product(held_back(chunk), first, place[:half])
            second = others + partner(others)
            if chunk + 1 < CHUNKS:
                following = early(chunk + 1, last)
            if waiting is not None:
                own_rows.append(hop(waiting, chunk - 1))
                waiting = None
            waiting = spread(chunk, lambda wanted: lax.select_n(slots[wanted], *first, *second))
            last = negative_product(parent_inverse, second, place[half:], last)
            blocks.append(summed(last))
        own_rows.append(hop(waiting, CHUNKS - 1))
    else:
        for chunk in range(CHUNKS):
            whole = lax.all_gather(cut(chunk), "row", axis=0, tiled=True)
            waiting = spread(
                chunk, lambda wanted: lax.dynamic_slice_in_dim(whole, wanted * block_rows, block_rows, 0)
            )
            own_rows.append(hop(waiting, chunk))
            last = negative_product(held_back(chunk), [whole], jnp.zeros((1,), jnp.int32))
            blocks.append(summed(last))
    own_rows = jnp.concatenate(own_rows, axis=1)
    grams = []
    for block in blocks:
        gram = lax.dot_general(
            own_rows,
            after(block, last),
            (((0,), (0,)), ((), ())),
            precision=lax.Precision.HIGH,
            preferred_element_type=jnp.float32,
        )
        grams.append(sum_over_row(gram, row_count))
    offdiag_block = jnp.concatenate(blocks, axis=1)
    diag_block = saved_diag - sum_over_col(jnp.concatenate(grams, axis=1), column_count)
    return offdiag_block, diag_block


def solution(mesh):
    in_specs = (P("row", "col"), P(("col", "row"), None), P("row", "col"))
    out_specs = (P(("row", "col"), None), P("row", "col"))
    return jax.shard_map(shards, mesh=mesh, in_specs=in_specs, out_specs=out_specs, check_vma=False)
```

```python
import functools

import jax
import jax.numpy as jnp
import numpy as np
from jax import lax
from jax.experimental import pallas as pl
from jax.experimental.pallas import tpu as pltpu
from jax.sharding import PartitionSpec as P

CHUNKS = 4
SPLITS = 2
LANES = 128
MIB = 1 << 20


def split(value):
    high = value.astype(jnp.bfloat16)
    low = (value - high.astype(jnp.float32)).astype(jnp.bfloat16)
    return high, low


def largest_divisor(extent, unit, limit):
    return max(d for d in range(unit, min(extent, limit) + 1, unit) if extent % d == 0)


def split_kernel(place_ref, *refs):
    del place_ref
    high_ref, low_ref = refs[-2:]
    count = high_ref.shape[1] // refs[0].shape[1]
    for slot, a_ref in enumerate(refs[:count]):
        span = pl.ds(slot * a_ref.shape[1], a_ref.shape[1])
        high_ref[:, span], low_ref[:, span] = split(a_ref[...])


def split_part(a, place, depth, part, given):
    rows = a.shape[0]
    count = place.shape[0]
    tile = largest_divisor(rows // SPLITS, 16, 256)
    steps = rows // SPLITS // tile
    a_specs = [
        pl.BlockSpec((tile, depth), lambda i, place, slot=slot: (part * steps + i, place[slot])) for slot in range(count)
    ]
    return pl.pallas_call(
        split_kernel,
        grid_spec=pltpu.PrefetchScalarGridSpec(
            num_scalar_prefetch=1,
            grid=(steps,),
            in_specs=a_specs + [pl.BlockSpec(memory_space=pl.ANY)] * len(given),
            out_specs=[pl.BlockSpec((tile, count * depth), lambda i, _: (part * steps + i, 0))] * 2,
        ),
        out_shape=[jax.ShapeDtypeStruct((rows, count * depth), jnp.bfloat16)] * 2,
        input_output_aliases={1 + count: 0, 2 + count: 1} if given else {},
        compiler_params=pltpu.CompilerParams(vmem_limit_bytes=24 * MIB, dimension_semantics=("arbitrary",)),
        cost_estimate=pl.CostEstimate(
            flops=2 * rows * depth * count // SPLITS,
            bytes_accessed=8 * rows * depth * count // SPLITS,
            transcendentals=0,
        ),
    )(place, *[a] * count, *given)


def product_kernel(count, ahead, place_ref, *refs):
    del place_ref
    a_count = 2 if ahead else count
    a_refs, pieces, sums = refs[:a_count], refs[a_count : a_count + count], refs[a_count + count : -2]
    out_ref, both_ref = refs[-2:]
    columns = out_ref.shape[1]
    depth = both_ref.shape[1]

    @pl.when(pl.program_id(0) == 0)
    def _():
        for slot, piece in enumerate(pieces):
            both_ref[slot, :, :columns], both_ref[slot, :, columns:] = split(-piece[...])

    dot = functools.partial(jnp.dot, preferred_element_type=jnp.float32)
    extent = largest_divisor(out_ref.shape[0], 16, 256)
    for first in range(0, out_ref.shape[0], extent):
        rows = pl.ds(first, extent)
        wide = narrow = None
        for slot in range(count):
            if ahead:
                high, low = (a_ref[rows, slot * depth : (slot + 1) * depth] for a_ref in a_refs)
            else:
                high, low = split(a_refs[slot][rows, :])
            terms = dot(high, both_ref[slot]), dot(low, both_ref[slot, :, :columns])
            wide, narrow = terms if wide is None else (wide + terms[0], narrow + terms[1])
        total = wide[:, :columns] + (wide[:, columns:] + narrow)
        out_ref[rows, :] = total + sums[0][rows, :] if sums else total


def negative_product(a, pieces, place=None, sums=None):
    ahead = place is None
    rows = a[0].shape[0] if ahead else a.shape[0]
    count = len(pieces)
    depth, columns = pieces[0].shape
    tile = largest_divisor(rows, 16, 512)
    out_spec = pl.BlockSpec((tile, columns), lambda i, _: (i, 0))
    if ahead:
        place = jnp.zeros((1,), jnp.int32)
        a_specs = [pl.BlockSpec((tile, depth * count), lambda i, _: (i, 0))] * 2
    else:
        a = [a] * count
        a_specs = [pl.BlockSpec((tile, depth), lambda i, place, slot=slot: (i, place[slot])) for slot in range(count)]
    whole = [pl.BlockSpec(piece.shape, lambda i, _: (0, 0), pipeline_mode=pl.Buffered(1)) for piece in pieces]
    given = [] if sums is None else [sums]
    return pl.pallas_call(
        functools.partial(product_kernel, count, ahead),
        grid_spec=pltpu.PrefetchScalarGridSpec(
            num_scalar_prefetch=1,
            grid=(rows // tile,),
            in_specs=a_specs + whole + [out_spec] * len(given),
            out_specs=out_spec,
            scratch_shapes=[pltpu.VMEM((count, depth, 2 * columns), jnp.bfloat16)],
        ),
        out_shape=jax.ShapeDtypeStruct((rows, columns), jnp.float32),
        compiler_params=pltpu.CompilerParams(vmem_limit_bytes=40 * MIB, dimension_semantics=("arbitrary",)),
        cost_estimate=pl.CostEstimate(
            flops=6 * rows * depth * count * columns,
            bytes_accessed=4 * (rows * depth * count + depth * count * columns + 2 * rows * columns),
            transcendentals=0,
        ),
    )(place, *a, *pieces, *given)


def gather_orders(count):
    masks = [1 << b for b in range(1, count.bit_length() - 1)]
    return list(zip(masks, masks[::-1]))


def gather_places(count):
    held = [[i] for i in range(count)]
    for masks in gather_orders(count):
        held = [held[i] + held[i ^ masks[i & 1]] for i in range(count)]
    half = count // 4
    both = [
        held[i][:half] + held[i ^ 1][:half] + held[i][half:] + held[i ^ 1][half:] for i in range(count)
    ]
    return np.array(both, np.int32)


def after(value, *others):
    return lax.optimization_barrier((value, *others))[0]


def cross(pieces, masks, count):
    pairs = [(i, i ^ masks[i & 1]) for i in range(count)]
    return [lax.ppermute(piece, "row", pairs) for piece in pieces]


def sum_over_row(value, count):
    rows, columns = value.shape
    me = lax.axis_index("row")
    value = value.reshape((2,) * (count.bit_length() - 1) + (rows // count, columns))
    for bit in range(count.bit_length() - 1):
        axis = value.ndim - 3
        mine = (me >> bit) & 1
        keep = lax.dynamic_index_in_dim(value, mine, axis, keepdims=False)
        send = lax.dynamic_index_in_dim(value, 1 - mine, axis, keepdims=False)
        value = keep + lax.ppermute(send, "row", [(i, i ^ (1 << bit)) for i in range(count)])
    return value


def sum_over_col(value, count):
    me = lax.axis_index("col")
    width = value.shape[1] // count
    total = lax.dynamic_slice_in_dim(value, me * width, width, 1)
    for shift in range(1, count):
        send = lax.dynamic_slice_in_dim(value, (me + shift) % count * width, width, 1)
        total = total + lax.ppermute(send, "col", [(i, (i + shift) % count) for i in range(count)])
    return total


def move(value, target):
    row_count, column_count = lax.axis_size("row"), lax.axis_size("col")
    pairs = []
    for r in range(row_count):
        for c in range(column_count):
            to_row, to_column = target(r, c)
            pairs.append((r * column_count + c, to_row * column_count + to_column))
    return lax.ppermute(value, ("row", "col"), pairs)


def shards(parent_inverse, panel, saved_diag):
    row_count, column_count = lax.axis_size("row"), lax.axis_size("col")
    row_index, column_index = lax.axis_index("row"), lax.axis_index("col")
    group = row_count // column_count
    block_rows = panel.shape[0]
    width = panel.shape[1] // CHUNKS
    stepwise = block_rows % LANES == 0
    orders = gather_orders(row_count)
    places = gather_places(row_count)
    place = jnp.asarray(places)[row_index]
    slots = jnp.asarray(np.argsort(places, axis=1).astype(np.int32))[row_index]

    def cut(chunk):
        return lax.slice_in_dim(panel, chunk * width, (chunk + 1) * width, axis=1)

    def partner(pieces):
        return cross(pieces, (1, 1), row_count)

    def early(chunk, last):
        pieces = [cut(chunk) if last is None else after(cut(chunk), last)]
        for masks in orders[:-1]:
            pieces = pieces + cross(pieces, masks, row_count)
        return pieces, pieces + partner(pieces)

    def spread(chunk, select):
        wanted = row_index % group * column_count + (column_index ^ (row_index // group) ^ (chunk % column_count))
        return move(select(wanted), lambda r, c: (r, c ^ (r // group) ^ (chunk % column_count)))

    def hop(value, chunk):
        return move(
            value, lambda r, c: (((r // group) ^ c ^ (chunk % column_count)) * group + r % group, c)
        )

    def summed(partial_block):
        return lax.psum_scatter(partial_block, "col", scatter_dimension=0, tiled=True)

    products, blocks, own_rows = [], [], []
    waiting = None
    last = None
    if stepwise:
        half = row_count // 2
        halves = ()
        for part in range(SPLITS):
            halves = split_part(parent_inverse, place[half:], block_rows, part, halves)
        following = early(0, None)
        for chunk in range(CHUNKS):
            mine, first = following
            others = cross([mine[0] if last is None else after(mine[0], last)] + mine[1:], orders[-1], row_count)
            last = negative_product(parent_inverse, first, place[:half])
            second = others + partner(others)
            if chunk + 1 < CHUNKS:
                following = early(chunk + 1, last)
            if waiting is not None:
                own_rows.append(hop(waiting, chunk - 1))
            waiting = spread(chunk, lambda wanted: lax.select_n(slots[wanted], *first, *second))
            last = negative_product(halves, second, sums=last)
            products.append(last)
            blocks.append(summed(last))
        own_rows.append(hop(waiting, CHUNKS - 1))
    else:
        for chunk in range(CHUNKS):
            whole = lax.all_gather(cut(chunk), "row", axis=0, tiled=True)
            waiting = spread(
                chunk, lambda wanted: lax.dynamic_slice_in_dim(whole, wanted * block_rows, block_rows, 0)
            )
            own_rows.append(hop(waiting, chunk))
            products.append(negative_product(parent_inverse, [whole], jnp.zeros((1,), jnp.int32)))
            blocks.append(summed(products[-1]))
    own_rows = jnp.concatenate(own_rows, axis=1)
    grams = []
    for chunk, block in enumerate(blocks):
        gram = lax.dot_general(
            own_rows,
            after(block, products[min(chunk + 2, CHUNKS - 1)]),
            (((0,), (0,)), ((), ())),
            precision=lax.Precision.HIGH,
            preferred_element_type=jnp.float32,
        )
        grams.append(sum_over_row(gram, row_count))
    offdiag_block = jnp.concatenate(blocks, axis=1)
    diag_block = saved_diag - sum_over_col(jnp.concatenate(grams, axis=1), column_count)
    return offdiag_block, diag_block


def solution(mesh):
    in_specs = (P("row", "col"), P(("col", "row"), None), P("row", "col"))
    out_specs = (P(("row", "col"), None), P("row", "col"))
    return jax.shard_map(shards, mesh=mesh, in_specs=in_specs, out_specs=out_specs, check_vma=False)
```

```python
import functools

import jax
import jax.numpy as jnp
import numpy as np
from jax import lax
from jax.experimental import pallas as pl
from jax.experimental.pallas import tpu as pltpu
from jax.sharding import PartitionSpec as P

CHUNKS = 4
LANES = 128
MIB = 1 << 20


def split(value):
    high = value.astype(jnp.bfloat16)
    low = (value - high.astype(jnp.float32)).astype(jnp.bfloat16)
    return high, low


def largest_divisor(extent, unit, limit):
    return max(d for d in range(unit, min(extent, limit) + 1, unit) if extent % d == 0)


def product_kernel(count, place_ref, *refs):
    del place_ref
    a_refs, pieces, sums, (out_ref, both_ref) = refs[:count], refs[count : 2 * count], refs[2 * count : -2], refs[-2:]
    columns = out_ref.shape[1]

    @pl.when(pl.program_id(0) == 0)
    def _():
        for slot, piece in enumerate(pieces):
            both_ref[slot, :, :columns], both_ref[slot, :, columns:] = split(-piece[...])

    dot = functools.partial(jnp.dot, preferred_element_type=jnp.float32)
    extent = largest_divisor(out_ref.shape[0], 16, 256)
    for first in range(0, out_ref.shape[0], extent):
        rows = pl.ds(first, extent)
        wide = narrow = None
        for slot in range(count):
            high, low = split(a_refs[slot][rows, :])
            terms = dot(high, both_ref[slot]), dot(low, both_ref[slot, :, :columns])
            wide, narrow = terms if wide is None else (wide + terms[0], narrow + terms[1])
        total = wide[:, :columns] + (wide[:, columns:] + narrow)
        out_ref[rows, :] = total + sums[0][rows, :] if sums else total


def negative_product(a, pieces, place, sums=None):
    rows = a.shape[0]
    count = len(pieces)
    depth, columns = pieces[0].shape
    tile = largest_divisor(rows, 16, 512)
    out_spec = pl.BlockSpec((tile, columns), lambda i, _: (i, 0))
    a_specs = [pl.BlockSpec((tile, depth), lambda i, place, slot=slot: (i, place[slot])) for slot in range(count)]
    whole = [pl.BlockSpec(piece.shape, lambda i, _: (0, 0), pipeline_mode=pl.Buffered(1)) for piece in pieces]
    given = [] if sums is None else [sums]
    return pl.pallas_call(
        functools.partial(product_kernel, count),
        grid_spec=pltpu.PrefetchScalarGridSpec(
            num_scalar_prefetch=1,
            grid=(rows // tile,),
            in_specs=a_specs + whole + [out_spec] * len(given),
            out_specs=out_spec,
            scratch_shapes=[pltpu.VMEM((count, depth, 2 * columns), jnp.bfloat16)],
        ),
        out_shape=jax.ShapeDtypeStruct((rows, columns), jnp.float32),
        compiler_params=pltpu.CompilerParams(vmem_limit_bytes=32 * MIB, dimension_semantics=("arbitrary",)),
        cost_estimate=pl.CostEstimate(
            flops=6 * rows * depth * count * columns,
            bytes_accessed=4 * (rows * depth * count + depth * count * columns + 2 * rows * columns),
            transcendentals=0,
        ),
    )(place, *[a] * count, *pieces, *given)


def gather_orders(count):
    masks = [1 << b for b in range(1, count.bit_length() - 1)]
    return list(zip(masks, masks[::-1]))


def gather_places(count):
    held = [[i] for i in range(count)]
    for masks in gather_orders(count):
        held = [held[i] + held[i ^ masks[i & 1]] for i in range(count)]
    half = count // 4
    both = [
        held[i][:half] + held[i ^ 1][:half] + held[i][half:] + held[i ^ 1][half:] for i in range(count)
    ]
    return np.array(both, np.int32)


def after(value, *others):
    return lax.optimization_barrier((value, *others))[0]


def cross(pieces, masks, count):
    pairs = [(i, i ^ masks[i & 1]) for i in range(count)]
    return [lax.ppermute(piece, "row", pairs) for piece in pieces]


def sum_over_row(value, count):
    rows, columns = value.shape
    me = lax.axis_index("row")
    value = value.reshape((2,) * (count.bit_length() - 1) + (rows // count, columns))
    for bit in range(count.bit_length() - 1):
        axis = value.ndim - 3
        mine = (me >> bit) & 1
        keep = lax.dynamic_index_in_dim(value, mine, axis, keepdims=False)
        send = lax.dynamic_index_in_dim(value, 1 - mine, axis, keepdims=False)
        value = keep + lax.ppermute(send, "row", [(i, i ^ (1 << bit)) for i in range(count)])
    return value


def sum_over_col(value, count):
    me = lax.axis_index("col")
    width = value.shape[1] // count
    total = lax.dynamic_slice_in_dim(value, me * width, width, 1)
    for shift in range(1, count):
        send = lax.dynamic_slice_in_dim(value, (me + shift) % count * width, width, 1)
        total = total + lax.ppermute(send, "col", [(i, (i + shift) % count) for i in range(count)])
    return total


def move(value, target):
    row_count, column_count = lax.axis_size("row"), lax.axis_size("col")
    pairs = []
    for r in range(row_count):
        for c in range(column_count):
            to_row, to_column = target(r, c)
            pairs.append((r * column_count + c, to_row * column_count + to_column))
    return lax.ppermute(value, ("row", "col"), pairs)


def shards(parent_inverse, panel, saved_diag):
    row_count, column_count = lax.axis_size("row"), lax.axis_size("col")
    row_index, column_index = lax.axis_index("row"), lax.axis_index("col")
    group = row_count // column_count
    block_rows = panel.shape[0]
    width = panel.shape[1] // CHUNKS
    stepwise = block_rows % LANES == 0
    orders = gather_orders(row_count)
    places = gather_places(row_count)
    place = jnp.asarray(places)[row_index]
    slots = jnp.asarray(np.argsort(places, axis=1).astype(np.int32))[row_index]

    def cut(chunk):
        return lax.slice_in_dim(panel, chunk * width, (chunk + 1) * width, axis=1)

    def partner(pieces):
        return cross(pieces, (1, 1), row_count)

    def all_after(pieces, *others):
        return [after(piece, *others) for piece in pieces]

    def turn(chunk):
        return chunk * 2 % column_count + chunk * 2 // column_count

    def spread(chunk, select):
        wanted = row_index % group * column_count + (column_index ^ (row_index // group) ^ turn(chunk))
        return move(select(wanted), lambda r, c: (r, c ^ (r // group) ^ turn(chunk)))

    def hop(value, chunk):
        return move(value, lambda r, c: (((r // group) ^ c ^ turn(chunk)) * group + r % group, c))

    def summed(partial_block, *others):
        return lax.psum_scatter(after(partial_block, *others), "col", scatter_dimension=0, tiled=True)

    products, blocks, moved = [], [], []
    if stepwise:
        half = row_count // 2

        def link(pieces, orders):
            for masks in orders:
                pieces = pieces + cross(pieces, masks, row_count)
            return pieces

        mine = [link([cut(0)], orders[:-1])] + [None] * (CHUNKS - 1)
        theirs = [partner(all_after(mine[0], mine[0][-1]))] + [None] * (CHUNKS - 1)
        late = [cross(all_after(mine[0], theirs[0][-1]), orders[-1], row_count)] + [None] * (CHUNKS - 1)
        mine[1] = link(all_after([cut(1)], late[0][-1]), orders[:-1])
        last = None
        for chunk in range(CHUNKS):
            if chunk == 1:
                theirs[1] = partner(all_after(mine[1], last))
                late[1] = cross(all_after(mine[1], theirs[1][-1]), orders[-1], row_count)
            if 1 <= chunk < CHUNKS - 1:
                mine[chunk + 1] = link(all_after([cut(chunk + 1)], last), orders[:-1])
            first = mine[chunk] + theirs[chunk]
            waits = moved[-1:]
            last = negative_product(after(parent_inverse, *waits) if waits else parent_inverse, first, place[:half])
            second = late[chunk] + partner(late[chunk])
            if 1 <= chunk < CHUNKS - 1:
                theirs[chunk + 1] = partner(all_after(mine[chunk + 1], last))
                late[chunk + 1] = cross(all_after(mine[chunk + 1], last), orders[-1], row_count)
            moved.append(spread(chunk, lambda wanted: lax.select_n(slots[wanted], *first, *second)))
            last = negative_product(parent_inverse, second, place[half:], last)
            products.append(last)
            if chunk == 0:
                waits = mine[1][-1:]
            elif chunk < CHUNKS - 1:
                waits = theirs[chunk + 1] + late[chunk + 1]
            else:
                waits = []
            blocks.append(summed(last, *waits))
        moved = [hop(after(value, products[-2]), chunk) for chunk, value in enumerate(moved)]
    else:
        for chunk in range(CHUNKS):
            whole = lax.all_gather(cut(chunk), "row", axis=0, tiled=True)
            part = spread(chunk, lambda wanted: lax.dynamic_slice_in_dim(whole, wanted * block_rows, block_rows, 0))
            moved.append(hop(part, chunk))
            products.append(negative_product(parent_inverse, [whole], jnp.zeros((1,), jnp.int32)))
            blocks.append(summed(products[-1]))
    own_rows = jnp.concatenate(moved, axis=1)
    grams = []
    for chunk, block in enumerate(blocks):
        waits = [products[-1]] if chunk < CHUNKS - 1 else grams
        gram = lax.dot_general(
            own_rows,
            after(block, *waits),
            (((0,), (0,)), ((), ())),
            precision=lax.Precision.HIGH,
            preferred_element_type=jnp.float32,
        )
        grams.append(sum_over_row(gram, row_count))
    offdiag_block = jnp.concatenate(blocks, axis=1)
    diag_block = saved_diag - sum_over_col(jnp.concatenate(grams, axis=1), column_count)
    return offdiag_block, diag_block


def solution(mesh):
    in_specs = (P("row", "col"), P(("col", "row"), None), P("row", "col"))
    out_specs = (P(("row", "col"), None), P("row", "col"))
    return jax.shard_map(shards, mesh=mesh, in_specs=in_specs, out_specs=out_specs, check_vma=False)
```

```python
import functools

import jax
import jax.numpy as jnp
import numpy as np
from jax import lax
from jax.experimental import pallas as pl
from jax.experimental.pallas import tpu as pltpu
from jax.sharding import PartitionSpec as P

CHUNKS = 2
SLICES = 4
LANES = 128
MIB = 1 << 20


def split(value):
    high = value.astype(jnp.bfloat16)
    low = (value - high.astype(jnp.float32)).astype(jnp.bfloat16)
    return high, low


def largest_divisor(extent, unit, limit):
    return max(d for d in range(unit, min(extent, limit) + 1, unit) if extent % d == 0)


def product_kernel(count, place_ref, *refs):
    del place_ref
    a_refs, pieces, sums, (out_ref, both_ref) = refs[:count], refs[count : 2 * count], refs[2 * count : -2], refs[-2:]
    columns = out_ref.shape[1]

    @pl.when(pl.program_id(0) == 0)
    def _():
        for slot, piece in enumerate(pieces):
            both_ref[slot, :, :columns], both_ref[slot, :, columns:] = split(-piece[...])

    dot = functools.partial(jnp.dot, preferred_element_type=jnp.float32)
    extent = largest_divisor(out_ref.shape[0], 16, 256)
    for first in range(0, out_ref.shape[0], extent):
        rows = pl.ds(first, extent)
        wide = narrow = None
        for slot in range(count):
            high, low = split(a_refs[slot][rows, :])
            terms = dot(high, both_ref[slot]), dot(low, both_ref[slot, :, :columns])
            wide, narrow = terms if wide is None else (wide + terms[0], narrow + terms[1])
        total = wide[:, :columns] + (wide[:, columns:] + narrow)
        out_ref[rows, :] = total + sums[0][rows, :] if sums else total


def negative_product(a, pieces, place, sums=None):
    rows = a.shape[0]
    count = len(pieces)
    depth, columns = pieces[0].shape
    tile = largest_divisor(rows, 16, 512)
    out_spec = pl.BlockSpec((tile, columns), lambda i, _: (i, 0))
    a_specs = [pl.BlockSpec((tile, depth), lambda i, place, slot=slot: (i, place[slot])) for slot in range(count)]
    whole = [pl.BlockSpec(piece.shape, lambda i, _: (0, 0), pipeline_mode=pl.Buffered(1)) for piece in pieces]
    given = [] if sums is None else [sums]
    return pl.pallas_call(
        functools.partial(product_kernel, count),
        grid_spec=pltpu.PrefetchScalarGridSpec(
            num_scalar_prefetch=1,
            grid=(rows // tile,),
            in_specs=a_specs + whole + [out_spec] * len(given),
            out_specs=out_spec,
            scratch_shapes=[pltpu.VMEM((count, depth, 2 * columns), jnp.bfloat16)],
        ),
        out_shape=jax.ShapeDtypeStruct((rows, columns), jnp.float32),
        compiler_params=pltpu.CompilerParams(vmem_limit_bytes=44 * MIB, dimension_semantics=("arbitrary",)),
        cost_estimate=pl.CostEstimate(
            flops=6 * rows * depth * count * columns,
            bytes_accessed=4 * (rows * depth * count + depth * count * columns + 2 * rows * columns),
            transcendentals=0,
        ),
    )(place, *[a] * count, *pieces, *given)


def gather_orders(count):
    masks = [1 << b for b in range(1, count.bit_length() - 1)]
    return list(zip(masks, masks[::-1]))


def gather_places(count):
    held = [[i] for i in range(count)]
    for masks in gather_orders(count):
        held = [held[i] + held[i ^ masks[i & 1]] for i in range(count)]
    half = count // 4
    both = [
        held[i][:half] + held[i ^ 1][:half] + held[i][half:] + held[i ^ 1][half:] for i in range(count)
    ]
    return np.array(both, np.int32)


def after(value, *others):
    return lax.optimization_barrier((value, *others))[0] if others else value


def cross(pieces, masks, count):
    pairs = [(i, i ^ masks[i & 1]) for i in range(count)]
    return [lax.ppermute(piece, "row", pairs) for piece in pieces]


def sum_over_row(value, count):
    rows, columns = value.shape
    me = lax.axis_index("row")
    value = value.reshape((2,) * (count.bit_length() - 1) + (rows // count, columns))
    for bit in range(count.bit_length() - 1):
        axis = value.ndim - 3
        mine = (me >> bit) & 1
        keep = lax.dynamic_index_in_dim(value, mine, axis, keepdims=False)
        send = lax.dynamic_index_in_dim(value, 1 - mine, axis, keepdims=False)
        value = keep + lax.ppermute(send, "row", [(i, i ^ (1 << bit)) for i in range(count)])
    return value


def sum_over_col(value, count):
    me = lax.axis_index("col")
    width = value.shape[1] // count
    total = lax.dynamic_slice_in_dim(value, me * width, width, 1)
    for shift in range(1, count):
        send = lax.dynamic_slice_in_dim(value, (me + shift) % count * width, width, 1)
        total = total + lax.ppermute(send, "col", [(i, (i + shift) % count) for i in range(count)])
    return total


def move(value, target, chosen):
    row_count, column_count = lax.axis_size("row"), lax.axis_size("col")
    pairs = []
    for r in range(row_count):
        for c in range(column_count):
            if chosen(r, c):
                to_row, to_column = target(r, c)
                pairs.append((r * column_count + c, to_row * column_count + to_column))
    return lax.ppermute(value, ("row", "col"), pairs)


def shards(parent_inverse, panel, saved_diag):
    row_count, column_count = lax.axis_size("row"), lax.axis_size("col")
    row_index = lax.axis_index("row")
    group = row_count // column_count
    width = panel.shape[1] // CHUNKS
    stepwise = panel.shape[0] % LANES == 0
    orders = gather_orders(row_count)
    place = jnp.asarray(gather_places(row_count))[row_index]

    def cut(chunk):
        return lax.slice_in_dim(panel, chunk * width, (chunk + 1) * width, axis=1)

    def partner(pieces):
        return cross(pieces, (1, 1), row_count)

    def all_after(pieces, *others):
        return [after(piece, *others) for piece in pieces]

    def over_col(part, flip):
        return [part] + [
            move(part, lambda r, c: (r ^ flip, r % column_count), lambda r, c: r % column_count ^ c == shift)
            for shift in range(1, column_count)
        ]

    def over_row(parts, flip):
        def arrived(part, shift, flip):
            return move(
                part,
                lambda r, c: ((c ^ shift) * group + (r ^ flip) // column_count, c),
                lambda r, c: (r ^ flip) % column_count == c,
            )

        found = [arrived(part, shift, flip if shift else 0) for shift, part in enumerate(parts)]
        return functools.reduce(jnp.add, found)

    def summed(partial_block, *others):
        return lax.psum_scatter(after(partial_block, *others), "col", scatter_dimension=0, tiled=True)

    breadth = panel.shape[1] // SLICES
    flips = [i % 2 * group for i in range(SLICES)]
    slices = [lax.slice_in_dim(panel, i * breadth, (i + 1) * breadth, axis=1) for i in range(SLICES)]
    products, blocks = [], []
    if stepwise:
        half = row_count // 2
        def link(pieces, orders):
            for masks in orders:
                pieces = pieces + cross(pieces, masks, row_count)
            return pieces

        mine = link([cut(0)], orders[:-1])
        pair = SLICES // 2
        moving = [over_col(part, flip) for part, flip in zip(slices[:pair], flips)]
        arrived = [part for parts in moving for part in parts[1:]]
        moving += [over_col(after(part, *arrived), flip) for part, flip in zip(slices[pair:], flips[pair:])]
        arrived = [arrived, [part for parts in moving[pair:] for part in parts[1:]]]
        last = None
        for chunk in range(CHUNKS):
            theirs = partner(all_after(mine, mine[-1]) if last is None else all_after(mine, last))
            late = cross(all_after(mine, theirs[-1]), orders[-1], row_count)
            last = negative_product(parent_inverse, mine + theirs, place[:half])
            waits = [last] if chunk else [last] + arrived[0]
            late = late + partner(all_after(late, *waits))
            if chunk + 1 < CHUNKS:
                mine = link(all_after([cut(chunk + 1)], last), orders[:-1])
            last = negative_product(parent_inverse, late, place[half:], last)
            products.append(last)
            waits = [] if chunk else arrived[1] + mine[-1:]
            blocks.append(summed(last, *waits))
        own_rows = [
            over_row([after(part, products[0]) for part in parts], flip) for parts, flip in zip(moving, flips)
        ]
    else:
        own_rows = [over_row(over_col(part, flip), flip) for part, flip in zip(slices, flips)]
        for chunk in range(CHUNKS):
            whole = lax.all_gather(cut(chunk), "row", axis=0, tiled=True)
            products.append(negative_product(parent_inverse, [whole], jnp.zeros((1,), jnp.int32)))
            blocks.append(summed(products[-1]))
    own_rows = jnp.concatenate(own_rows, axis=1)
    grams = []
    for chunk, block in enumerate(blocks):
        waits = [products[-1]] if chunk < CHUNKS - 1 else grams
        gram = lax.dot_general(
            own_rows,
            after(block, *waits),
            (((0,), (0,)), ((), ())),
            precision=lax.Precision.HIGH,
            preferred_element_type=jnp.float32,
        )
        grams.append(sum_over_row(gram, row_count))
    offdiag_block = jnp.concatenate(blocks, axis=1)
    diag_block = saved_diag - sum_over_col(jnp.concatenate(grams, axis=1), column_count)
    return offdiag_block, diag_block


def solution(mesh):
    in_specs = (P("row", "col"), P(("col", "row"), None), P("row", "col"))
    out_specs = (P(("row", "col"), None), P("row", "col"))
    return jax.shard_map(shards, mesh=mesh, in_specs=in_specs, out_specs=out_specs, check_vma=False)
```

```python
import functools

import jax
import jax.numpy as jnp
import numpy as np
from jax import lax
from jax.experimental import pallas as pl
from jax.experimental.pallas import tpu as pltpu
from jax.sharding import PartitionSpec as P

EIGHTHS = (3, 3, 2)
LANES = 128
MIB = 1 << 20


def split(value):
    high = value.astype(jnp.bfloat16)
    low = (value - high.astype(jnp.float32)).astype(jnp.bfloat16)
    return high, low


def largest_divisor(extent, unit, limit):
    return max(d for d in range(unit, min(extent, limit) + 1, unit) if extent % d == 0)


def product_kernel(count, place_ref, *refs):
    del place_ref
    a_refs, pieces, sums, (out_ref, both_ref) = refs[:count], refs[count : 2 * count], refs[2 * count : -2], refs[-2:]
    columns = out_ref.shape[1]

    @pl.when(pl.program_id(0) == 0)
    def _():
        for slot, piece in enumerate(pieces):
            both_ref[slot, :, :columns], both_ref[slot, :, columns:] = split(-piece[...])

    dot = functools.partial(jnp.dot, preferred_element_type=jnp.float32)
    extent = largest_divisor(out_ref.shape[0], 16, 256)
    for first in range(0, out_ref.shape[0], extent):
        rows = pl.ds(first, extent)
        wide = narrow = None
        for slot in range(count):
            high, low = split(a_refs[slot][rows, :])
            terms = dot(high, both_ref[slot]), dot(low, both_ref[slot, :, :columns])
            wide, narrow = terms if wide is None else (wide + terms[0], narrow + terms[1])
        total = wide[:, :columns] + (wide[:, columns:] + narrow)
        out_ref[rows, :] = total + sums[0][rows, :] if sums else total


def negative_product(a, pieces, place, sums=None):
    rows = a.shape[0]
    count = len(pieces)
    depth, columns = pieces[0].shape
    tile = largest_divisor(rows, 16, 512)
    out_spec = pl.BlockSpec((tile, columns), lambda i, _: (i, 0))
    a_specs = [pl.BlockSpec((tile, depth), lambda i, place, slot=slot: (i, place[slot])) for slot in range(count)]
    whole = [pl.BlockSpec(piece.shape, lambda i, _: (0, 0), pipeline_mode=pl.Buffered(1)) for piece in pieces]
    given = [] if sums is None else [sums]
    return pl.pallas_call(
        functools.partial(product_kernel, count),
        grid_spec=pltpu.PrefetchScalarGridSpec(
            num_scalar_prefetch=1,
            grid=(rows // tile,),
            in_specs=a_specs + whole + [out_spec] * len(given),
            out_specs=out_spec,
            scratch_shapes=[pltpu.VMEM((count, depth, 2 * columns), jnp.bfloat16)],
        ),
        out_shape=jax.ShapeDtypeStruct((rows, columns), jnp.float32),
        compiler_params=pltpu.CompilerParams(vmem_limit_bytes=44 * MIB, dimension_semantics=("arbitrary",)),
        cost_estimate=pl.CostEstimate(
            flops=6 * rows * depth * count * columns,
            bytes_accessed=4 * (rows * depth * count + depth * count * columns + 2 * rows * columns),
            transcendentals=0,
        ),
    )(place, *[a] * count, *pieces, *given)


def gather_orders(count):
    masks = [1 << b for b in range(1, count.bit_length() - 1)]
    return list(zip(masks, masks[::-1]))


def gather_places(count):
    held = [[i] for i in range(count)]
    for masks in gather_orders(count):
        held = [held[i] + held[i ^ masks[i & 1]] for i in range(count)]
    half = count // 4
    both = [
        held[i][:half] + held[i ^ 1][:half] + held[i][half:] + held[i ^ 1][half:] for i in range(count)
    ]
    return np.array(both, np.int32)


def after(value, *others):
    return lax.optimization_barrier((value, *others))[0] if others else value


def cross(pieces, masks, count):
    pairs = [(i, i ^ masks[i & 1]) for i in range(count)]
    return [lax.ppermute(piece, "row", pairs) for piece in pieces]


def sum_over_row(value, count):
    rows, columns = value.shape
    me = lax.axis_index("row")
    value = value.reshape((2,) * (count.bit_length() - 1) + (rows // count, columns))
    for bit in range(count.bit_length() - 1):
        axis = value.ndim - 3
        mine = (me >> bit) & 1
        keep = lax.dynamic_index_in_dim(value, mine, axis, keepdims=False)
        send = lax.dynamic_index_in_dim(value, 1 - mine, axis, keepdims=False)
        value = keep + lax.ppermute(send, "row", [(i, i ^ (1 << bit)) for i in range(count)])
    return value


def sum_over_col(value, count):
    me = lax.axis_index("col")
    width = value.shape[1] // count
    total = lax.dynamic_slice_in_dim(value, me * width, width, 1)
    for shift in range(1, count):
        send = lax.dynamic_slice_in_dim(value, (me + shift) % count * width, width, 1)
        total = total + lax.ppermute(send, "col", [(i, (i + shift) % count) for i in range(count)])
    return total


def move(value, target):
    row_count, column_count = lax.axis_size("row"), lax.axis_size("col")
    pairs = []
    for r in range(row_count):
        for c in range(column_count):
            to = target(r, c)
            if to is not None:
                pairs.append((r * column_count + c, to[0] * column_count + to[1]))
    return lax.ppermute(value, ("row", "col"), pairs)


def shards(parent_inverse, panel, saved_diag):
    row_count, column_count = lax.axis_size("row"), lax.axis_size("col")
    row_index, column_index = lax.axis_index("row"), lax.axis_index("col")
    group = row_count // column_count
    stepwise = panel.shape[0] % LANES == 0
    orders = gather_orders(row_count)
    place = jnp.asarray(gather_places(row_count))[row_index]
    unit = panel.shape[1] // 8
    chunks, first = [], 0
    for size in EIGHTHS:
        chunks.append(lax.slice_in_dim(panel, first * unit, (first + size) * unit, axis=1))
        first += size

    def partner(pieces):
        return cross(pieces, (1, 1), row_count)

    def all_after(pieces, *others):
        return [after(piece, *others) for piece in pieces]

    rounds = [(k, k % (column_count - 1) + 1) for k in range(1, column_count)]
    panel_left, panel_right = jnp.split(panel, 2, axis=1)

    def over_col(shifts, *others):
        left, right = shifts

        def target(r, c):
            goal = r % column_count
            return {left: (r, goal), right: (r ^ group, goal)}.get(goal ^ c)

        sends_right = (row_index % column_count) ^ column_index == right
        return move(after(jnp.where(sends_right, panel_right, panel_left), *others), target)

    def over_row(arrived):
        def target(left, right):
            def of(r, c):
                for source, shift in ((r, left), (r ^ group, right)):
                    if source % column_count == c:
                        return (c ^ shift) * group + source // column_count, c

            return of

        def still(r, c):
            return (c * group + r // column_count, c) if r % column_count == c else None

        halves = list(jnp.split(move(panel, still), 2, axis=1))
        mine = (row_index // group) ^ column_index
        for value, shifts in zip(arrived, rounds):
            value = move(value, target(*shifts))
            for side in range(2):
                halves[side] = halves[side] + jnp.where(mine == shifts[side], value, jnp.zeros_like(value))
        return jnp.concatenate(halves, axis=1)

    def summed(partial_block, *others):
        return lax.psum_scatter(after(partial_block, *others), "col", scatter_dimension=0, tiled=True)

    products, blocks = [], []
    if stepwise:
        half = row_count // 2

        def link(pieces, orders):
            for masks in orders:
                pieces = pieces + cross(pieces, masks, row_count)
            return pieces

        mine = link(chunks[:1], orders[:-1])
        arrived = [over_col(shifts, mine[-1]) for shifts in rounds[:2]]
        arrived += [over_col(shifts, *arrived) for shifts in rounds[2:]]
        last = None
        for chunk in range(len(chunks)):
            theirs = partner(all_after(mine, mine[-1]) if last is None else all_after(mine, last))
            late = cross(all_after(mine, theirs[-1]), orders[-1], row_count)
            last = negative_product(parent_inverse, mine + theirs, place[:half])
            waits = [last] if chunk else [last] + arrived[:2]
            late = late + partner(all_after(late, *waits))
            if chunk + 1 < len(chunks):
                mine = link(all_after([chunks[chunk + 1]], last), orders[:-1])
            last = negative_product(parent_inverse, late, place[half:], last)
            products.append(last)
            waits = mine[-1:] if chunk + 1 < len(chunks) else []
            blocks.append(summed(last, *waits, *([] if chunk else arrived[2:])))
        own_rows = over_row([after(value, products[0]) for value in arrived])
    else:
        own_rows = over_row([over_col(shifts) for shifts in rounds])
        for own in chunks:
            whole = lax.all_gather(own, "row", axis=0, tiled=True)
            products.append(negative_product(parent_inverse, [whole], jnp.zeros((1,), jnp.int32)))
            blocks.append(summed(products[-1]))
    grams = []
    for chunk, block in enumerate(blocks):
        waits = [products[-1]] if chunk < len(blocks) - 1 else grams
        gram = lax.dot_general(
            own_rows,
            after(block, *waits),
            (((0,), (0,)), ((), ())),
            precision=lax.Precision.HIGH,
            preferred_element_type=jnp.float32,
        )
        grams.append(sum_over_row(gram, row_count))
    offdiag_block = jnp.concatenate(blocks, axis=1)
    diag_block = saved_diag - sum_over_col(jnp.concatenate(grams, axis=1), column_count)
    return offdiag_block, diag_block


def solution(mesh):
    in_specs = (P("row", "col"), P(("col", "row"), None), P("row", "col"))
    out_specs = (P(("row", "col"), None), P("row", "col"))
    return jax.shard_map(shards, mesh=mesh, in_specs=in_specs, out_specs=out_specs, check_vma=False)
```

```python
import functools

import jax
import jax.numpy as jnp
import numpy as np
from jax import lax
from jax.experimental import pallas as pl
from jax.experimental.pallas import tpu as pltpu
from jax.sharding import PartitionSpec as P

EIGHTHS = (3, 3, 2)
LANES = 128
MIB = 1 << 20


def split(value):
    high = value.astype(jnp.bfloat16)
    low = (value - high.astype(jnp.float32)).astype(jnp.bfloat16)
    return high, low


def largest_divisor(extent, unit, limit):
    return max(d for d in range(unit, min(extent, limit) + 1, unit) if extent % d == 0)


def product_kernel(count, place_ref, *refs):
    del place_ref
    a_refs, pieces, sums, (out_ref, both_ref) = refs[:count], refs[count : 2 * count], refs[2 * count : -2], refs[-2:]
    columns = out_ref.shape[1]

    @pl.when(pl.program_id(0) == 0)
    def _():
        for slot, piece in enumerate(pieces):
            both_ref[slot, :, :columns], both_ref[slot, :, columns:] = split(-piece[...])

    dot = functools.partial(jnp.dot, preferred_element_type=jnp.float32)
    extent = largest_divisor(out_ref.shape[0], 16, 256)
    for first in range(0, out_ref.shape[0], extent):
        rows = pl.ds(first, extent)
        wide = narrow = None
        for slot in range(count):
            high, low = split(a_refs[slot][rows, :])
            terms = dot(high, both_ref[slot]), dot(low, both_ref[slot, :, :columns])
            wide, narrow = terms if wide is None else (wide + terms[0], narrow + terms[1])
        total = wide[:, :columns] + (wide[:, columns:] + narrow)
        out_ref[rows, :] = total + sums[0][rows, :] if sums else total


def negative_product(a, pieces, place, sums=None):
    rows = a.shape[0]
    count = len(pieces)
    depth, columns = pieces[0].shape
    tile = largest_divisor(rows, 16, 512)
    out_spec = pl.BlockSpec((tile, columns), lambda i, _: (i, 0))
    a_specs = [pl.BlockSpec((tile, depth), lambda i, place, slot=slot: (i, place[slot])) for slot in range(count)]
    whole = [pl.BlockSpec(piece.shape, lambda i, _: (0, 0), pipeline_mode=pl.Buffered(1)) for piece in pieces]
    given = [] if sums is None else [sums]
    return pl.pallas_call(
        functools.partial(product_kernel, count),
        grid_spec=pltpu.PrefetchScalarGridSpec(
            num_scalar_prefetch=1,
            grid=(rows // tile,),
            in_specs=a_specs + whole + [out_spec] * len(given),
            out_specs=out_spec,
            scratch_shapes=[pltpu.VMEM((count, depth, 2 * columns), jnp.bfloat16)],
        ),
        out_shape=jax.ShapeDtypeStruct((rows, columns), jnp.float32),
        compiler_params=pltpu.CompilerParams(vmem_limit_bytes=44 * MIB, dimension_semantics=("arbitrary",)),
        cost_estimate=pl.CostEstimate(
            flops=6 * rows * depth * count * columns,
            bytes_accessed=4 * (rows * depth * count + depth * count * columns + 2 * rows * columns),
            transcendentals=0,
        ),
    )(place, *[a] * count, *pieces, *given)


def gather_orders(count):
    masks = [1 << b for b in range(1, count.bit_length() - 1)]
    return list(zip(masks, masks[::-1]))


def gather_places(count):
    held = [[i] for i in range(count)]
    for masks in gather_orders(count):
        held = [held[i] + held[i ^ masks[i & 1]] for i in range(count)]
    half = count // 4
    both = [
        held[i][:half] + held[i ^ 1][:half] + held[i][half:] + held[i ^ 1][half:] for i in range(count)
    ]
    return np.array(both, np.int32)


def after(value, *others):
    return lax.optimization_barrier((value, *others))[0] if others else value


def cross(pieces, masks, count):
    pairs = [(i, i ^ masks[i & 1]) for i in range(count)]
    return [lax.ppermute(piece, "row", pairs) for piece in pieces]


def sum_over_row(value, count):
    rows, columns = value.shape
    me = lax.axis_index("row")
    value = value.reshape((2,) * (count.bit_length() - 1) + (rows // count, columns))
    for bit in range(count.bit_length() - 1):
        axis = value.ndim - 3
        mine = (me >> bit) & 1
        keep = lax.dynamic_index_in_dim(value, mine, axis, keepdims=False)
        send = lax.dynamic_index_in_dim(value, 1 - mine, axis, keepdims=False)
        value = keep + lax.ppermute(send, "row", [(i, i ^ (1 << bit)) for i in range(count)])
    return value


def sum_over_col(value, count):
    me = lax.axis_index("col")
    width = value.shape[1] // count
    total = lax.dynamic_slice_in_dim(value, me * width, width, 1)
    for shift in range(1, count):
        send = lax.dynamic_slice_in_dim(value, (me + shift) % count * width, width, 1)
        total = total + lax.ppermute(send, "col", [(i, (i + shift) % count) for i in range(count)])
    return total


def move(value, target):
    row_count, column_count = lax.axis_size("row"), lax.axis_size("col")
    pairs = []
    for r in range(row_count):
        for c in range(column_count):
            to = target(r, c)
            if to is not None:
                pairs.append((r * column_count + c, to[0] * column_count + to[1]))
    return lax.ppermute(value, ("row", "col"), pairs)


def shards(parent_inverse, panel, saved_diag):
    row_count, column_count = lax.axis_size("row"), lax.axis_size("col")
    row_index, column_index = lax.axis_index("row"), lax.axis_index("col")
    group = row_count // column_count
    stepwise = panel.shape[0] % LANES == 0
    orders = gather_orders(row_count)
    place = jnp.asarray(gather_places(row_count))[row_index]
    unit = panel.shape[1] // 8
    chunks, first = [], 0
    for size in EIGHTHS:
        chunks.append(lax.slice_in_dim(panel, first * unit, (first + size) * unit, axis=1))
        first += size

    def partner(pieces):
        return cross(pieces, (1, 1), row_count)

    def all_after(pieces, *others):
        return [after(piece, *others) for piece in pieces]

    panel_left, panel_right = jnp.split(panel, 2, axis=1)
    to_goal = (row_index % column_count) ^ column_index

    def right_of_neighbour():
        return move(panel_right, lambda r, c: (r ^ group, c))

    def over_col(right, k, *others):
        def target(r, c):
            return (r, c ^ k) if r % column_count ^ c in (k, k ^ group) else None

        return move(after(jnp.where(to_goal == k, panel_left, right), *others), target)

    def over_row(right, arrived):
        left_parts, right_parts = [panel_left, *arrived], [right, *arrived]
        mine = (row_index // group) ^ column_index
        halves = [jnp.zeros_like(panel_left)] * 2
        for k in range(column_count):
            other = (k + 1) % column_count

            def target(r, c):
                shift = {c: k, c ^ group: other}.get(r % column_count)
                return None if shift is None else ((c ^ shift) * group + r // column_count, c)

            value = move(jnp.where(to_goal == 0, left_parts[k], right_parts[other]), target)
            halves = [jnp.where(mine == shift, value, held) for shift, held in zip((k, other), halves)]
        return jnp.concatenate(halves, axis=1)

    def summed(partial_block, *others):
        return lax.psum_scatter(after(partial_block, *others), "col", scatter_dimension=0, tiled=True)

    products, blocks = [], []
    if stepwise:
        half = row_count // 2

        def link(pieces, orders):
            for masks in orders:
                pieces = pieces + cross(pieces, masks, row_count)
            return pieces

        mine = link(chunks[:1], orders[:-1])
        right = right_of_neighbour()
        arrived = [over_col(right, k) for k in range(1, min(3, column_count))]
        early = len(arrived)
        arrived += [over_col(right, k, *arrived) for k in range(3, column_count)]
        last = None
        for chunk in range(len(chunks)):
            theirs = partner(all_after(mine, mine[-1]) if last is None else all_after(mine, last))
            late = cross(all_after(mine, theirs[-1]), orders[-1], row_count)
            last = negative_product(parent_inverse, mine + theirs, place[:half])
            waits = [last] if chunk else [last] + arrived[:early]
            late = late + partner(all_after(late, *waits))
            if chunk + 1 < len(chunks):
                mine = link(all_after([chunks[chunk + 1]], last), orders[:-1])
            last = negative_product(parent_inverse, late, place[half:], last)
            products.append(last)
            waits = mine[-1:] if chunk + 1 < len(chunks) else []
            blocks.append(summed(last, *waits, *([] if chunk else arrived[early:])))
        own_rows = over_row(right, [after(value, products[0]) for value in arrived])
    else:
        right = right_of_neighbour()
        own_rows = over_row(right, [over_col(right, k) for k in range(1, column_count)])
        for own in chunks:
            whole = lax.all_gather(own, "row", axis=0, tiled=True)
            products.append(negative_product(parent_inverse, [whole], jnp.zeros((1,), jnp.int32)))
            blocks.append(summed(products[-1]))
    grams = []
    for chunk, block in enumerate(blocks):
        waits = [products[-1]] if chunk < len(blocks) - 1 else grams
        gram = lax.dot_general(
            own_rows,
            after(block, *waits),
            (((0,), (0,)), ((), ())),
            precision=lax.Precision.HIGH,
            preferred_element_type=jnp.float32,
        )
        grams.append(sum_over_row(gram, row_count))
    offdiag_block = jnp.concatenate(blocks, axis=1)
    diag_block = saved_diag - sum_over_col(jnp.concatenate(grams, axis=1), column_count)
    return offdiag_block, diag_block


def solution(mesh):
    in_specs = (P("row", "col"), P(("col", "row"), None), P("row", "col"))
    out_specs = (P(("row", "col"), None), P("row", "col"))
    return jax.shard_map(shards, mesh=mesh, in_specs=in_specs, out_specs=out_specs, check_vma=False)
```

```python
import functools

import jax
import jax.numpy as jnp
import numpy as np
from jax import lax
from jax.experimental import pallas as pl
from jax.experimental.pallas import tpu as pltpu
from jax.sharding import PartitionSpec as P

EIGHTHS = (2, 2, 3, 1)
LANES = 128
MIB = 1 << 20


def split(value):
    high = value.astype(jnp.bfloat16)
    low = (value - high.astype(jnp.float32)).astype(jnp.bfloat16)
    return high, low


def largest_divisor(extent, unit, limit):
    return max(d for d in range(unit, min(extent, limit) + 1, unit) if extent % d == 0)


def product_kernel(count, place_ref, *refs):
    del place_ref
    a_refs, pieces, sums, (out_ref, both_ref) = refs[:count], refs[count : 2 * count], refs[2 * count : -2], refs[-2:]
    columns = out_ref.shape[1]

    @pl.when(pl.program_id(0) == 0)
    def _():
        for slot, piece in enumerate(pieces):
            both_ref[slot, :, :columns], both_ref[slot, :, columns:] = split(-piece[...])

    dot = functools.partial(jnp.dot, preferred_element_type=jnp.float32)
    extent = largest_divisor(out_ref.shape[0], 16, 256)
    for first in range(0, out_ref.shape[0], extent):
        rows = pl.ds(first, extent)
        wide = narrow = None
        for slot in range(count):
            high, low = split(a_refs[slot][rows, :])
            terms = dot(high, both_ref[slot]), dot(low, both_ref[slot, :, :columns])
            wide, narrow = terms if wide is None else (wide + terms[0], narrow + terms[1])
        total = wide[:, :columns] + (wide[:, columns:] + narrow)
        out_ref[rows, :] = total + sums[0][rows, :] if sums else total


def negative_product(a, pieces, place, sums=None):
    rows = a.shape[0]
    count = len(pieces)
    depth, columns = pieces[0].shape
    tile = largest_divisor(rows, 16, 512)
    out_spec = pl.BlockSpec((tile, columns), lambda i, _: (i, 0))
    a_specs = [pl.BlockSpec((tile, depth), lambda i, place, slot=slot: (i, place[slot])) for slot in range(count)]
    whole = [pl.BlockSpec(piece.shape, lambda i, _: (0, 0), pipeline_mode=pl.Buffered(1)) for piece in pieces]
    given = [] if sums is None else [sums]
    return pl.pallas_call(
        functools.partial(product_kernel, count),
        grid_spec=pltpu.PrefetchScalarGridSpec(
            num_scalar_prefetch=1,
            grid=(rows // tile,),
            in_specs=a_specs + whole + [out_spec] * len(given),
            out_specs=out_spec,
            scratch_shapes=[pltpu.VMEM((count, depth, 2 * columns), jnp.bfloat16)],
        ),
        out_shape=jax.ShapeDtypeStruct((rows, columns), jnp.float32),
        compiler_params=pltpu.CompilerParams(vmem_limit_bytes=44 * MIB, dimension_semantics=("arbitrary",)),
        cost_estimate=pl.CostEstimate(
            flops=6 * rows * depth * count * columns,
            bytes_accessed=4 * (rows * depth * count + depth * count * columns + 2 * rows * columns),
            transcendentals=0,
        ),
    )(place, *[a] * count, *pieces, *given)


def gather_orders(count):
    masks = [1 << b for b in range(1, count.bit_length() - 1)]
    return list(zip(masks, masks[::-1]))


def gather_places(count):
    held = [[i] for i in range(count)]
    for masks in gather_orders(count):
        held = [held[i] + held[i ^ masks[i & 1]] for i in range(count)]
    half = count // 4
    both = [
        held[i][:half] + held[i ^ 1][:half] + held[i][half:] + held[i ^ 1][half:] for i in range(count)
    ]
    return np.array(both, np.int32)


def after(value, *others):
    return lax.optimization_barrier((value, *others))[0] if others else value


def cross(pieces, masks, count):
    pairs = [(i, i ^ masks[i & 1]) for i in range(count)]
    return [lax.ppermute(piece, "row", pairs) for piece in pieces]


def sum_over_row(value, count):
    rows, columns = value.shape
    chips = count // 2
    me = lax.axis_index("row")
    core, chip = me % 2, me // 2
    value = value.reshape(chips, 2, rows // count, columns)
    keep = lax.dynamic_index_in_dim(value, core, 1, keepdims=False)
    send = lax.dynamic_index_in_dim(value, 1 - core, 1, keepdims=False)
    value = keep + lax.ppermute(send, "row", [(i, i ^ 1) for i in range(count)])
    total = lax.dynamic_index_in_dim(value, chip, 0, keepdims=False)
    for mask in range(1, chips):
        send = lax.dynamic_index_in_dim(value, chip ^ mask, 0, keepdims=False)
        total = total + lax.ppermute(send, "row", [(i, i ^ (2 * mask)) for i in range(count)])
    return total


def sum_over_col(value, count):
    me = lax.axis_index("col")
    width = value.shape[1] // count
    total = lax.dynamic_slice_in_dim(value, me * width, width, 1)
    for shift in range(1, count):
        send = lax.dynamic_slice_in_dim(value, (me + shift) % count * width, width, 1)
        total = total + lax.ppermute(send, "col", [(i, (i + shift) % count) for i in range(count)])
    return total


def move(value, target):
    row_count, column_count = lax.axis_size("row"), lax.axis_size("col")
    pairs = []
    for r in range(row_count):
        for c in range(column_count):
            to = target(r, c)
            if to is not None:
                pairs.append((r * column_count + c, to[0] * column_count + to[1]))
    return lax.ppermute(value, ("row", "col"), pairs)


def shards(parent_inverse, panel, saved_diag):
    row_count, column_count = lax.axis_size("row"), lax.axis_size("col")
    row_index, column_index = lax.axis_index("row"), lax.axis_index("col")
    group = row_count // column_count
    stepwise = panel.shape[0] % LANES == 0
    orders = gather_orders(row_count)
    place = jnp.asarray(gather_places(row_count))[row_index]
    unit = panel.shape[1] // 8
    chunks, first = [], 0
    for size in EIGHTHS:
        chunks.append(lax.slice_in_dim(panel, first * unit, (first + size) * unit, axis=1))
        first += size

    def partner(pieces):
        return cross(pieces, (1, 1), row_count)

    def all_after(pieces, *others):
        return [after(piece, *others) for piece in pieces]

    panel_left, panel_right = jnp.split(panel, 2, axis=1)
    to_goal = (row_index % column_count) ^ column_index

    def to_neighbour(value):
        return move(value, lambda r, c: (r ^ group, c))

    def over_col(left, k, *others):
        def target(r, c):
            return (r, c ^ k) if r % column_count ^ c in (k, k ^ group) else None

        return move(after(jnp.where(to_goal == k, panel_right, left), *others), target)

    def over_row(left, arrived):
        right_parts, left_parts = [panel_right, *arrived], [left, *arrived]
        mine = (row_index // group) ^ column_index
        halves = [jnp.zeros_like(panel_left)] * 2
        for k in range(column_count):
            other = (k + 1) % column_count

            def target(r, c):
                shift = {c: k, c ^ group: other}.get(r % column_count)
                return None if shift is None else ((c ^ shift) * group + r // column_count, c)

            value = move(jnp.where(to_goal == 0, right_parts[k], left_parts[other]), target)
            halves = [jnp.where(mine == shift, value, held) for shift, held in zip((other, k), halves)]
        return jnp.concatenate(halves, axis=1)

    def summed(partial_block, *others):
        return lax.psum_scatter(after(partial_block, *others), "col", scatter_dimension=0, tiled=True)

    products, blocks = [], []
    if stepwise:
        half = row_count // 2

        def link(pieces, orders):
            for masks in orders:
                pieces = pieces + cross(pieces, masks, row_count)
            return pieces

        mine = link(chunks[:1], orders[:-1])
        hopped = to_neighbour(panel_left[:, chunks[0].shape[1] :])
        last = None
        for chunk in range(len(chunks)):
            theirs = partner(all_after(mine, mine[-1]) if last is None else all_after(mine, last))
            late = cross(all_after(mine, theirs[-1], *([] if chunk else [hopped])), orders[-1], row_count)
            last = negative_product(parent_inverse, mine + theirs, place[:half])
            if chunk == 0:
                left = jnp.concatenate([jnp.where(row_index % 2 == 0, mine[1], late[0]), hopped], axis=1)
                arrived = [over_col(left, k) for k in range(1, min(3, column_count))]
                early = len(arrived)
                arrived += [over_col(left, k, *arrived) for k in range(3, column_count)]
            late = late + partner(all_after(late, last, *(arrived[early:] if chunk == 1 else [])))
            if chunk + 1 < len(chunks):
                mine = link(all_after([chunks[chunk + 1]], last), orders[:-1])
            last = negative_product(parent_inverse, late, place[half:], last)
            products.append(last)
            waits = mine[-1:] if chunk + 1 < len(chunks) else []
            blocks.append(summed(last, *waits, *([] if chunk else arrived[:early])))
        own_rows = over_row(left, [after(value, products[1]) for value in arrived])
    else:
        left = to_neighbour(panel_left)
        own_rows = over_row(left, [over_col(left, k) for k in range(1, column_count)])
        for own in chunks:
            whole = lax.all_gather(own, "row", axis=0, tiled=True)
            products.append(negative_product(parent_inverse, [whole], jnp.zeros((1,), jnp.int32)))
            blocks.append(summed(products[-1]))
    grams = []
    for chunk, block in enumerate(blocks):
        waits = [products[-1]] if chunk < len(blocks) - 1 else grams
        gram = lax.dot_general(
            own_rows,
            after(block, *waits),
            (((0,), (0,)), ((), ())),
            precision=lax.Precision.HIGH,
            preferred_element_type=jnp.float32,
        )
        grams.append(sum_over_row(gram, row_count))
    offdiag_block = jnp.concatenate(blocks, axis=1)
    diag_block = saved_diag - sum_over_col(jnp.concatenate(grams, axis=1), column_count)
    return offdiag_block, diag_block


def solution(mesh):
    in_specs = (P("row", "col"), P(("col", "row"), None), P("row", "col"))
    out_specs = (P(("row", "col"), None), P("row", "col"))
    return jax.shard_map(shards, mesh=mesh, in_specs=in_specs, out_specs=out_specs, check_vma=False)
```

```python
import functools

import jax
import jax.numpy as jnp
import numpy as np
from jax import lax
from jax.experimental import pallas as pl
from jax.experimental.pallas import tpu as pltpu
from jax.sharding import PartitionSpec as P

EIGHTHS = (2, 3, 3)
LANES = 128
MIB = 1 << 20


def split(value):
    high = value.astype(jnp.bfloat16)
    low = (value - high.astype(jnp.float32)).astype(jnp.bfloat16)
    return high, low


def largest_divisor(extent, unit, limit):
    return max(d for d in range(unit, min(extent, limit) + 1, unit) if extent % d == 0)


def product_kernel(count, place_ref, *refs):
    del place_ref
    a_refs, pieces, sums, (out_ref, both_ref) = refs[:count], refs[count : 2 * count], refs[2 * count : -2], refs[-2:]
    columns = out_ref.shape[1]

    @pl.when(pl.program_id(0) == 0)
    def _():
        for slot, piece in enumerate(pieces):
            both_ref[slot, :, :columns], both_ref[slot, :, columns:] = split(-piece[...])

    dot = functools.partial(jnp.dot, preferred_element_type=jnp.float32)
    extent = largest_divisor(out_ref.shape[0], 16, 256)
    for first in range(0, out_ref.shape[0], extent):
        rows = pl.ds(first, extent)
        wide = narrow = None
        for slot in range(count):
            high, low = split(a_refs[slot][rows, :])
            terms = dot(high, both_ref[slot]), dot(low, both_ref[slot, :, :columns])
            wide, narrow = terms if wide is None else (wide + terms[0], narrow + terms[1])
        total = wide[:, :columns] + (wide[:, columns:] + narrow)
        out_ref[rows, :] = total + sums[0][rows, :] if sums else total


def negative_product(a, pieces, place, sums=None):
    rows = a.shape[0]
    count = len(pieces)
    depth, columns = pieces[0].shape
    tile = largest_divisor(rows, 16, 512)
    out_spec = pl.BlockSpec((tile, columns), lambda i, _: (i, 0))
    a_specs = [pl.BlockSpec((tile, depth), lambda i, place, slot=slot: (i, place[slot])) for slot in range(count)]
    whole = [pl.BlockSpec(piece.shape, lambda i, _: (0, 0), pipeline_mode=pl.Buffered(1)) for piece in pieces]
    given = [] if sums is None else [sums]
    return pl.pallas_call(
        functools.partial(product_kernel, count),
        grid_spec=pltpu.PrefetchScalarGridSpec(
            num_scalar_prefetch=1,
            grid=(rows // tile,),
            in_specs=a_specs + whole + [out_spec] * len(given),
            out_specs=out_spec,
            scratch_shapes=[pltpu.VMEM((count, depth, 2 * columns), jnp.bfloat16)],
        ),
        out_shape=jax.ShapeDtypeStruct((rows, columns), jnp.float32),
        compiler_params=pltpu.CompilerParams(vmem_limit_bytes=44 * MIB, dimension_semantics=("arbitrary",)),
        cost_estimate=pl.CostEstimate(
            flops=6 * rows * depth * count * columns,
            bytes_accessed=4 * (rows * depth * count + depth * count * columns + 2 * rows * columns),
            transcendentals=0,
        ),
    )(place, *[a] * count, *pieces, *given)


def gather_orders(count):
    masks = [1 << b for b in range(1, count.bit_length() - 1)]
    return list(zip(masks, masks[::-1]))


def gather_places(count):
    held = [[i] for i in range(count)]
    for masks in gather_orders(count):
        held = [held[i] + held[i ^ masks[i & 1]] for i in range(count)]
    half = count // 4
    both = [
        held[i][:half] + held[i ^ 1][:half] + held[i][half:] + held[i ^ 1][half:] for i in range(count)
    ]
    return np.array(both, np.int32)


def after(value, *others):
    return lax.optimization_barrier((value, *others))[0] if others else value


def cross(pieces, masks, count):
    pairs = [(i, i ^ masks[i & 1]) for i in range(count)]
    return [lax.ppermute(piece, "row", pairs) for piece in pieces]


def sum_over_row(value, count):
    rows, columns = value.shape
    chips = count // 2
    me = lax.axis_index("row")
    core, chip = me % 2, me // 2
    value = value.reshape(chips, 2, rows // count, columns)
    keep = lax.dynamic_index_in_dim(value, core, 1, keepdims=False)
    send = lax.dynamic_index_in_dim(value, 1 - core, 1, keepdims=False)
    value = keep + lax.ppermute(send, "row", [(i, i ^ 1) for i in range(count)])
    total = lax.dynamic_index_in_dim(value, chip, 0, keepdims=False)
    for mask in range(1, chips):
        send = lax.dynamic_index_in_dim(value, chip ^ mask, 0, keepdims=False)
        total = total + lax.ppermute(send, "row", [(i, i ^ (2 * mask)) for i in range(count)])
    return total


def sum_over_col(value, count):
    me = lax.axis_index("col")
    width = value.shape[1] // count
    total = lax.dynamic_slice_in_dim(value, me * width, width, 1)
    for shift in range(1, count):
        send = lax.dynamic_slice_in_dim(value, (me + shift) % count * width, width, 1)
        total = total + lax.ppermute(send, "col", [(i, (i + shift) % count) for i in range(count)])
    return total


def move(value, target):
    row_count, column_count = lax.axis_size("row"), lax.axis_size("col")
    pairs = []
    for r in range(row_count):
        for c in range(column_count):
            to = target(r, c)
            if to is not None:
                pairs.append((r * column_count + c, to[0] * column_count + to[1]))
    return lax.ppermute(value, ("row", "col"), pairs)


def shards(parent_inverse, panel, saved_diag):
    row_count, column_count = lax.axis_size("row"), lax.axis_size("col")
    row_index, column_index = lax.axis_index("row"), lax.axis_index("col")
    group = row_count // column_count
    stepwise = panel.shape[0] % LANES == 0
    orders = gather_orders(row_count)
    place = jnp.asarray(gather_places(row_count))[row_index]
    unit = panel.shape[1] // 8
    chunks, first = [], 0
    for size in EIGHTHS:
        chunks.append(lax.slice_in_dim(panel, first * unit, (first + size) * unit, axis=1))
        first += size

    def partner(pieces):
        return cross(pieces, (1, 1), row_count)

    def all_after(pieces, *others):
        return [after(piece, *others) for piece in pieces]

    panel_left, panel_right = jnp.split(panel, 2, axis=1)
    to_goal = (row_index % column_count) ^ column_index

    def right_of_neighbour():
        return move(panel_right, lambda r, c: (r ^ group, c))

    def over_col(right, k, *others):
        def target(r, c):
            return (r, c ^ k) if r % column_count ^ c in (k, k ^ group) else None

        return move(after(jnp.where(to_goal == k, panel_left, right), *others), target)

    def over_row(right, arrived):
        left_parts, right_parts = [panel_left, *arrived], [right, *arrived]
        mine = (row_index // group) ^ column_index
        halves = [jnp.zeros_like(panel_left)] * 2
        for k in range(column_count):
            other = (k + 1) % column_count

            def target(r, c):
                shift = {c: k, c ^ group: other}.get(r % column_count)
                return None if shift is None else ((c ^ shift) * group + r // column_count, c)

            value = move(jnp.where(to_goal == 0, left_parts[k], right_parts[other]), target)
            halves = [jnp.where(mine == shift, value, held) for shift, held in zip((k, other), halves)]
        return jnp.concatenate(halves, axis=1)

    def summed(partial_block, *others):
        return lax.psum_scatter(after(partial_block, *others), "col", scatter_dimension=0, tiled=True)

    products, blocks = [], []
    if stepwise:
        half = row_count // 2

        def link(pieces, orders):
            for masks in orders:
                pieces = pieces + cross(pieces, masks, row_count)
            return pieces

        right = right_of_neighbour()
        mine = link(all_after(chunks[:1], right), orders[:-1])
        arrived = [over_col(right, k) for k in range(1, min(3, column_count))]
        early = len(arrived)
        arrived += [over_col(right, k, *arrived) for k in range(3, column_count)]
        last = None
        for chunk in range(len(chunks)):
            theirs = partner(all_after(mine, mine[-1]) if last is None else all_after(mine, last))
            late = cross(all_after(mine, theirs[-1]), orders[-1], row_count)
            last = negative_product(parent_inverse, mine + theirs, place[:half])
            waits = [last] if chunk else [last] + arrived[:early]
            late = late + partner(all_after(late, *waits))
            if chunk + 1 < len(chunks):
                mine = link(all_after([chunks[chunk + 1]], last), orders[:-1])
            last = negative_product(parent_inverse, late, place[half:], last)
            products.append(last)
            waits = mine[-1:] if chunk + 1 < len(chunks) else []
            blocks.append(summed(last, *waits, *([] if chunk else arrived[early:])))
        own_rows = over_row(right, [after(value, products[-1]) for value in arrived])
    else:
        right = right_of_neighbour()
        own_rows = over_row(right, [over_col(right, k) for k in range(1, column_count)])
        for own in chunks:
            whole = lax.all_gather(own, "row", axis=0, tiled=True)
            products.append(negative_product(parent_inverse, [whole], jnp.zeros((1,), jnp.int32)))
            blocks.append(summed(products[-1]))
    grams = []
    for chunk, block in enumerate(blocks):
        waits = [products[-1]] if chunk < len(blocks) - 1 else grams
        gram = lax.dot_general(
            own_rows,
            after(block, *waits),
            (((0,), (0,)), ((), ())),
            precision=lax.Precision.HIGH,
            preferred_element_type=jnp.float32,
        )
        grams.append(sum_over_row(gram, row_count))
    offdiag_block = jnp.concatenate(blocks, axis=1)
    diag_block = saved_diag - sum_over_col(jnp.concatenate(grams, axis=1), column_count)
    return offdiag_block, diag_block


def solution(mesh):
    in_specs = (P("row", "col"), P(("col", "row"), None), P("row", "col"))
    out_specs = (P(("row", "col"), None), P("row", "col"))
    return jax.shard_map(shards, mesh=mesh, in_specs=in_specs, out_specs=out_specs, check_vma=False)
```

```python
import functools

import jax
import jax.numpy as jnp
import numpy as np
from jax import lax
from jax.experimental import pallas as pl
from jax.experimental.pallas import tpu as pltpu
from jax.sharding import PartitionSpec as P

EIGHTHS = (3, 3, 2)
LANES = 128
MIB = 1 << 20


def split(value):
    high = value.astype(jnp.bfloat16)
    low = (value - high.astype(jnp.float32)).astype(jnp.bfloat16)
    return high, low


def largest_divisor(extent, unit, limit):
    return max(d for d in range(unit, min(extent, limit) + 1, unit) if extent % d == 0)


def product_kernel(count, place_ref, *refs):
    del place_ref
    a_refs, pieces, sums, (out_ref, both_ref) = refs[:count], refs[count : 2 * count], refs[2 * count : -2], refs[-2:]
    columns = out_ref.shape[1]

    @pl.when(pl.program_id(0) == 0)
    def _():
        for slot, piece in enumerate(pieces):
            both_ref[slot, :, :columns], both_ref[slot, :, columns:] = split(-piece[...])

    dot = functools.partial(jnp.dot, preferred_element_type=jnp.float32)
    extent = largest_divisor(out_ref.shape[0], 16, 256)
    for first in range(0, out_ref.shape[0], extent):
        rows = pl.ds(first, extent)
        wide = narrow = None
        for slot in range(count):
            high, low = split(a_refs[slot][rows, :])
            terms = dot(high, both_ref[slot]), dot(low, both_ref[slot, :, :columns])
            wide, narrow = terms if wide is None else (wide + terms[0], narrow + terms[1])
        total = wide[:, :columns] + (wide[:, columns:] + narrow)
        out_ref[rows, :] = total + sums[0][rows, :] if sums else total


def negative_product(a, pieces, place, sums=None):
    rows = a.shape[0]
    count = len(pieces)
    depth, columns = pieces[0].shape
    tile = largest_divisor(rows, 16, 512)
    out_spec = pl.BlockSpec((tile, columns), lambda i, _: (i, 0))
    a_specs = [pl.BlockSpec((tile, depth), lambda i, place, slot=slot: (i, place[slot])) for slot in range(count)]
    whole = [pl.BlockSpec(piece.shape, lambda i, _: (0, 0), pipeline_mode=pl.Buffered(1)) for piece in pieces]
    given = [] if sums is None else [sums]
    return pl.pallas_call(
        functools.partial(product_kernel, count),
        grid_spec=pltpu.PrefetchScalarGridSpec(
            num_scalar_prefetch=1,
            grid=(rows // tile,),
            in_specs=a_specs + whole + [out_spec] * len(given),
            out_specs=out_spec,
            scratch_shapes=[pltpu.VMEM((count, depth, 2 * columns), jnp.bfloat16)],
        ),
        out_shape=jax.ShapeDtypeStruct((rows, columns), jnp.float32),
        compiler_params=pltpu.CompilerParams(vmem_limit_bytes=44 * MIB, dimension_semantics=("arbitrary",)),
        cost_estimate=pl.CostEstimate(
            flops=6 * rows * depth * count * columns,
            bytes_accessed=4 * (rows * depth * count + depth * count * columns + 2 * rows * columns),
            transcendentals=0,
        ),
    )(place, *[a] * count, *pieces, *given)


def gather_orders(count):
    masks = [1 << b for b in range(1, count.bit_length() - 1)]
    return list(zip(masks[::-1], masks[::-1])), list(zip(masks, masks[::-1]))


def gather_places(count, orders):
    held = [[i] for i in range(count)]
    for masks in orders:
        held = [held[i] + held[i ^ masks[i & 1]] for i in range(count)]
    half = count // 4
    both = [
        held[i][:half] + held[i ^ 1][:half] + held[i][half:] + held[i ^ 1][half:] for i in range(count)
    ]
    return np.array(both, np.int32)


def after(value, *others):
    return lax.optimization_barrier((value, *others))[0] if others else value


def cross(pieces, masks, count):
    pairs = [(i, i ^ masks[i & 1]) for i in range(count)]
    return [lax.ppermute(piece, "row", pairs) for piece in pieces]


def sum_over_row(value, count):
    rows, columns = value.shape
    chips = count // 2
    me = lax.axis_index("row")
    core, chip = me % 2, me // 2
    value = value.reshape(chips, 2, rows // count, columns)
    keep = lax.dynamic_index_in_dim(value, core, 1, keepdims=False)
    send = lax.dynamic_index_in_dim(value, 1 - core, 1, keepdims=False)
    value = keep + lax.ppermute(send, "row", [(i, i ^ 1) for i in range(count)])
    total = lax.dynamic_index_in_dim(value, chip, 0, keepdims=False)
    for mask in range(1, chips):
        send = lax.dynamic_index_in_dim(value, chip ^ mask, 0, keepdims=False)
        total = total + lax.ppermute(send, "row", [(i, i ^ (2 * mask)) for i in range(count)])
    return total


def sum_over_col(value, count):
    me = lax.axis_index("col")
    width = value.shape[1] // count
    total = lax.dynamic_slice_in_dim(value, me * width, width, 1)
    for shift in range(1, count):
        send = lax.dynamic_slice_in_dim(value, (me + shift) % count * width, width, 1)
        total = total + lax.ppermute(send, "col", [(i, (i + shift) % count) for i in range(count)])
    return total


def move(value, target):
    row_count, column_count = lax.axis_size("row"), lax.axis_size("col")
    pairs = []
    for r in range(row_count):
        for c in range(column_count):
            to = target(r, c)
            if to is not None:
                pairs.append((r * column_count + c, to[0] * column_count + to[1]))
    return lax.ppermute(value, ("row", "col"), pairs)


def shards(parent_inverse, panel, saved_diag):
    row_count, column_count = lax.axis_size("row"), lax.axis_size("col")
    row_index, column_index = lax.axis_index("row"), lax.axis_index("col")
    group = row_count // column_count
    stepwise = panel.shape[0] % LANES == 0
    first_orders, later_orders = gather_orders(row_count)
    places = [jnp.asarray(gather_places(row_count, orders))[row_index] for orders in (first_orders, later_orders)]
    unit = panel.shape[1] // 8
    chunks, first = [], 0
    for size in EIGHTHS:
        chunks.append(lax.slice_in_dim(panel, first * unit, (first + size) * unit, axis=1))
        first += size

    def partner(pieces):
        return cross(pieces, (1, 1), row_count)

    def all_after(pieces, *others):
        return [after(piece, *others) for piece in pieces]

    panel_left, panel_right = jnp.split(panel, 2, axis=1)
    to_goal = (row_index % column_count) ^ column_index

    def right_of_neighbour():
        return move(panel_right, lambda r, c: (r ^ group, c))

    def over_col(right, k, *others):
        def target(r, c):
            return (r, c ^ k) if r % column_count ^ c in (k, k ^ group) else None

        return move(after(jnp.where(to_goal == k, panel_left, right), *others), target)

    def over_row(right, arrived):
        left_parts, right_parts = [panel_left, *arrived], [right, *arrived]
        mine = (row_index // group) ^ column_index
        halves = [jnp.zeros_like(panel_left)] * 2
        for k in range(column_count):
            other = (k + 1) % column_count

            def target(r, c):
                shift = {c: k, c ^ group: other}.get(r % column_count)
                return None if shift is None else ((c ^ shift) * group + r // column_count, c)

            value = move(jnp.where(to_goal == 0, left_parts[k], right_parts[other]), target)
            halves = [jnp.where(mine == shift, value, held) for shift, held in zip((k, other), halves)]
        return jnp.concatenate(halves, axis=1)

    def summed(partial_block, *others):
        return lax.psum_scatter(after(partial_block, *others), "col", scatter_dimension=0, tiled=True)

    products, blocks = [], []
    if stepwise:
        half = row_count // 2

        def link(pieces, orders):
            for masks in orders:
                pieces = pieces + cross(pieces, masks, row_count)
            return pieces

        mine = link(chunks[:1], first_orders[:-1])
        right = right_of_neighbour()
        arrived = [over_col(right, k) for k in range(1, min(3, column_count))]
        early = len(arrived)
        arrived += [over_col(right, k, *arrived) for k in range(3, column_count)]
        last = None
        for chunk in range(len(chunks)):
            place, orders = (places[1], later_orders) if chunk else (places[0], first_orders)
            theirs = partner(all_after(mine, mine[-1]) if last is None else all_after(mine, last))
            late = cross(all_after(mine, theirs[-1]), orders[-1], row_count)
            last = negative_product(parent_inverse, mine + theirs, place[:half])
            waits = [last] if chunk else [last] + arrived[:early]
            late = late + partner(all_after(late, *waits))
            if chunk + 1 < len(chunks):
                mine = link(all_after([chunks[chunk + 1]], last), later_orders[:-1])
            last = negative_product(parent_inverse, late, place[half:], last)
            products.append(last)
            waits = mine[-1:] if chunk + 1 < len(chunks) else []
            blocks.append(summed(last, *waits, *([] if chunk else arrived[early:])))
        own_rows = over_row(right, [after(value, products[0]) for value in arrived])
    else:
        right = right_of_neighbour()
        own_rows = over_row(right, [over_col(right, k) for k in range(1, column_count)])
        for own in chunks:
            whole = lax.all_gather(own, "row", axis=0, tiled=True)
            products.append(negative_product(parent_inverse, [whole], jnp.zeros((1,), jnp.int32)))
            blocks.append(summed(products[-1]))
    grams = []
    for chunk, block in enumerate(blocks):
        waits = [products[-1]] if chunk < len(blocks) - 1 else grams
        gram = lax.dot_general(
            own_rows,
            after(block, *waits),
            (((0,), (0,)), ((), ())),
            precision=lax.Precision.HIGH,
            preferred_element_type=jnp.float32,
        )
        grams.append(sum_over_row(gram, row_count))
    offdiag_block = jnp.concatenate(blocks, axis=1)
    diag_block = saved_diag - sum_over_col(jnp.concatenate(grams, axis=1), column_count)
    return offdiag_block, diag_block


def solution(mesh):
    in_specs = (P("row", "col"), P(("col", "row"), None), P("row", "col"))
    out_specs = (P(("row", "col"), None), P("row", "col"))
    return jax.shard_map(shards, mesh=mesh, in_specs=in_specs, out_specs=out_specs, check_vma=False)
```

```python
import functools

import jax
import jax.numpy as jnp
import numpy as np
from jax import lax
from jax.experimental import pallas as pl
from jax.experimental.pallas import tpu as pltpu
from jax.sharding import PartitionSpec as P

EIGHTHS = (2, 2, 2, 2)
LANES = 128
MIB = 1 << 20


def split(value):
    high = value.astype(jnp.bfloat16)
    low = (value - high.astype(jnp.float32)).astype(jnp.bfloat16)
    return high, low


def largest_divisor(extent, unit, limit):
    return max(d for d in range(unit, min(extent, limit) + 1, unit) if extent % d == 0)


def product_kernel(count, place_ref, *refs):
    del place_ref
    a_refs, pieces, sums, (out_ref, both_ref) = refs[:count], refs[count : 2 * count], refs[2 * count : -2], refs[-2:]
    columns = out_ref.shape[1]

    @pl.when(pl.program_id(0) == 0)
    def _():
        for slot, piece in enumerate(pieces):
            both_ref[slot, :, :columns], both_ref[slot, :, columns:] = split(-piece[...])

    dot = functools.partial(jnp.dot, preferred_element_type=jnp.float32)
    extent = largest_divisor(out_ref.shape[0], 16, 256)
    for first in range(0, out_ref.shape[0], extent):
        rows = pl.ds(first, extent)
        wide = narrow = None
        for slot in range(count):
            high, low = split(a_refs[slot][rows, :])
            terms = dot(high, both_ref[slot]), dot(low, both_ref[slot, :, :columns])
            wide, narrow = terms if wide is None else (wide + terms[0], narrow + terms[1])
        total = wide[:, :columns] + (wide[:, columns:] + narrow)
        out_ref[rows, :] = total + sums[0][rows, :] if sums else total


def negative_product(a, pieces, place, sums=None):
    rows = a.shape[0]
    count = len(pieces)
    depth, columns = pieces[0].shape
    tile = largest_divisor(rows, 16, 512)
    out_spec = pl.BlockSpec((tile, columns), lambda i, _: (i, 0))
    a_specs = [pl.BlockSpec((tile, depth), lambda i, place, slot=slot: (i, place[slot])) for slot in range(count)]
    whole = [pl.BlockSpec(piece.shape, lambda i, _: (0, 0), pipeline_mode=pl.Buffered(1)) for piece in pieces]
    given = [] if sums is None else [sums]
    return pl.pallas_call(
        functools.partial(product_kernel, count),
        grid_spec=pltpu.PrefetchScalarGridSpec(
            num_scalar_prefetch=1,
            grid=(rows // tile,),
            in_specs=a_specs + whole + [out_spec] * len(given),
            out_specs=out_spec,
            scratch_shapes=[pltpu.VMEM((count, depth, 2 * columns), jnp.bfloat16)],
        ),
        out_shape=jax.ShapeDtypeStruct((rows, columns), jnp.float32),
        compiler_params=pltpu.CompilerParams(vmem_limit_bytes=44 * MIB, dimension_semantics=("arbitrary",)),
        cost_estimate=pl.CostEstimate(
            flops=6 * rows * depth * count * columns,
            bytes_accessed=4 * (rows * depth * count + depth * count * columns + 2 * rows * columns),
            transcendentals=0,
        ),
    )(place, *[a] * count, *pieces, *given)


def gather_orders(count):
    masks = [1 << b for b in range(1, count.bit_length() - 1)]
    return list(zip(masks[::-1], masks[::-1])), list(zip(masks, masks[::-1]))


def gather_places(count, orders):
    held = [[i] for i in range(count)]
    for masks in orders:
        held = [held[i] + held[i ^ masks[i & 1]] for i in range(count)]
    half = count // 4
    both = [
        held[i][:half] + held[i ^ 1][:half] + held[i][half:] + held[i ^ 1][half:] for i in range(count)
    ]
    return np.array(both, np.int32)


def after(value, *others):
    return lax.optimization_barrier((value, *others))[0] if others else value


def cross(pieces, masks, count):
    pairs = [(i, i ^ masks[i & 1]) for i in range(count)]
    return [lax.ppermute(piece, "row", pairs) for piece in pieces]


def sum_over_row(value, count):
    rows, columns = value.shape
    chips = count // 2
    me = lax.axis_index("row")
    core, chip = me % 2, me // 2
    value = value.reshape(chips, 2, rows // count, columns)
    keep = lax.dynamic_index_in_dim(value, core, 1, keepdims=False)
    send = lax.dynamic_index_in_dim(value, 1 - core, 1, keepdims=False)
    value = keep + lax.ppermute(send, "row", [(i, i ^ 1) for i in range(count)])
    total = lax.dynamic_index_in_dim(value, chip, 0, keepdims=False)
    for mask in range(1, chips):
        send = lax.dynamic_index_in_dim(value, chip ^ mask, 0, keepdims=False)
        total = total + lax.ppermute(send, "row", [(i, i ^ (2 * mask)) for i in range(count)])
    return total


def sum_over_col(value, count):
    me = lax.axis_index("col")
    width = value.shape[1] // count
    total = lax.dynamic_slice_in_dim(value, me * width, width, 1)
    for shift in range(1, count):
        send = lax.dynamic_slice_in_dim(value, (me + shift) % count * width, width, 1)
        total = total + lax.ppermute(send, "col", [(i, (i + shift) % count) for i in range(count)])
    return total


def move(value, target):
    row_count, column_count = lax.axis_size("row"), lax.axis_size("col")
    pairs = []
    for r in range(row_count):
        for c in range(column_count):
            to = target(r, c)
            if to is not None:
                pairs.append((r * column_count + c, to[0] * column_count + to[1]))
    return lax.ppermute(value, ("row", "col"), pairs)


def shards(parent_inverse, panel, saved_diag):
    row_count, column_count = lax.axis_size("row"), lax.axis_size("col")
    row_index, column_index = lax.axis_index("row"), lax.axis_index("col")
    group = row_count // column_count
    stepwise = panel.shape[0] % LANES == 0
    first_orders, later_orders = gather_orders(row_count)
    places = [jnp.asarray(gather_places(row_count, orders))[row_index] for orders in (first_orders, later_orders)]
    unit = panel.shape[1] // 8
    chunks, first = [], 0
    for size in EIGHTHS:
        chunks.append(lax.slice_in_dim(panel, first * unit, (first + size) * unit, axis=1))
        first += size

    def partner(pieces):
        return cross(pieces, (1, 1), row_count)

    def all_after(pieces, *others):
        return [after(piece, *others) for piece in pieces]

    panel_left, panel_right = jnp.split(panel, 2, axis=1)
    to_goal = (row_index % column_count) ^ column_index

    def right_of_neighbour():
        return move(panel_right, lambda r, c: (r ^ group, c))

    def over_col(right, k, *others):
        def target(r, c):
            return (r, c ^ k) if r % column_count ^ c in (k, k ^ group) else None

        return move(after(jnp.where(to_goal == k, panel_left, right), *others), target)

    def over_row(right, arrived):
        left_parts, right_parts = [panel_left, *arrived], [right, *arrived]
        mine = (row_index // group) ^ column_index
        halves = [jnp.zeros_like(panel_left)] * 2
        for k in range(column_count):
            other = (k + 1) % column_count

            def target(r, c):
                shift = {c: k, c ^ group: other}.get(r % column_count)
                return None if shift is None else ((c ^ shift) * group + r // column_count, c)

            value = move(jnp.where(to_goal == 0, left_parts[k], right_parts[other]), target)
            halves = [jnp.where(mine == shift, value, held) for shift, held in zip((k, other), halves)]
        return jnp.concatenate(halves, axis=1)

    def summed(partial_block, *others):
        return lax.psum_scatter(after(partial_block, *others), "col", scatter_dimension=0, tiled=True)

    products, blocks = [], []
    if stepwise:
        half = row_count // 2

        def link(pieces, orders):
            for masks in orders:
                pieces = pieces + cross(pieces, masks, row_count)
            return pieces

        mine = link(chunks[:1], first_orders[:-1])
        right = right_of_neighbour()
        arrived = [over_col(right, k) for k in range(1, min(3, column_count))]
        early = len(arrived)
        arrived += [over_col(right, k, *arrived) for k in range(3, column_count)]
        last = None
        for chunk in range(len(chunks)):
            place, orders = (places[1], later_orders) if chunk else (places[0], first_orders)
            theirs = partner(all_after(mine, mine[-1]) if last is None else all_after(mine, last))
            late = cross(all_after(mine, theirs[-1]), orders[-1], row_count)
            last = negative_product(parent_inverse, mine + theirs, place[:half])
            waits = [last] if chunk else [last] + arrived[:early]
            late = late + partner(all_after(late, *waits))
            if chunk + 1 < len(chunks):
                mine = link(all_after([chunks[chunk + 1]], last), later_orders[:-1])
            last = negative_product(parent_inverse, late, place[half:], last)
            products.append(last)
            waits = mine[-1:] if chunk + 1 < len(chunks) else []
            blocks.append(summed(last, *waits, *([] if chunk else arrived[early:])))
        own_rows = over_row(right, [after(value, products[-1]) for value in arrived])
    else:
        right = right_of_neighbour()
        own_rows = over_row(right, [over_col(right, k) for k in range(1, column_count)])
        for own in chunks:
            whole = lax.all_gather(own, "row", axis=0, tiled=True)
            products.append(negative_product(parent_inverse, [whole], jnp.zeros((1,), jnp.int32)))
            blocks.append(summed(products[-1]))
    grams = []
    for chunk, block in enumerate(blocks):
        waits = [products[-1]] if chunk < len(blocks) - 1 else grams
        gram = lax.dot_general(
            own_rows,
            after(block, *waits),
            (((0,), (0,)), ((), ())),
            precision=lax.Precision.HIGH,
            preferred_element_type=jnp.float32,
        )
        grams.append(sum_over_row(gram, row_count))
    offdiag_block = jnp.concatenate(blocks, axis=1)
    diag_block = saved_diag - sum_over_col(jnp.concatenate(grams, axis=1), column_count)
    return offdiag_block, diag_block


def solution(mesh):
    in_specs = (P("row", "col"), P(("col", "row"), None), P("row", "col"))
    out_specs = (P(("row", "col"), None), P("row", "col"))
    return jax.shard_map(shards, mesh=mesh, in_specs=in_specs, out_specs=out_specs, check_vma=False)
```
